32 devices in a mesh: dp: 8 (over z, x), expert: 4 (over y, core).
Axes of the slice: x: 2, y: 2, z: 4, core: 2. Of those that a mesh axis runs over, the one named last changes fastest.
Arguments:
- saved_inputs: bfloat16 [8, 4, 1024, 4096], P('dp', 'expert'), may hold values from -6 to 6
- saved_grads: bfloat16 [8, 4, 1024, 1536], P('dp', 'expert'), may hold values from -6 to 6
- row_counts: int32 [8, 4], P('dp', 'expert'), may hold values from 1 to 1024, as said below
- row_seq: int32 [8, 4, 1024], P('dp', 'expert'), may hold values from 0 to 255
- proj_in: bfloat16 [4096, 32], replicated, may hold values from -0.09375 to 0.09375
- proj_out: bfloat16 [1536, 32], replicated, may hold values from -0.15625 to 0.15625
Outputs:
- logged: bfloat16 [4, 2048, 1024], P(None, ('dp', 'expert'))
- fisher: float32 [1024, 4, 1024], P('dp', 'expert')
The draws below stay inside these ranges and needn't reach their ends.
Inputs may be any that keep to these rules, and one draw needn't show every extreme that they name: Slots from row_counts on are padding with arbitrary contents; row_counts reaches 1024 for some expert in every draw.
All inputs are finite; a program needn't handle non-finite values.
Results may differ from the reference program's by a relative error of at most 0.012.
Values may be sent and summed in bfloat16 or wider, within the bound.
A program may use at most 64 MiB of HBM per device.

```python
import jax
import jax.numpy as jnp
from jax import lax

D = 4096
FF = 1536
K = 32
CAP = 1024
SEQ_DEV = 256
EXPERTS = 4
N_DP = 8


def draw_row_counts(key, part):
    key_fill = jax.random.fold_in(key, 11)
    key_star = jax.random.fold_in(key, 23)
    shard_ids = jnp.arange(N_DP, dtype=jnp.int32)[:, None]
    top_count = CAP - 2 * CAP // 3 * (N_DP - 1 - shard_ids) // max(N_DP - 1, 1)
    low_count = jnp.maximum(top_count // 4, 1)
    raw_bits = jax.random.randint(key_fill, (N_DP, EXPERTS), 0, 1 << 20)
    counts = low_count + raw_bits % (top_count - low_count + 1)
    star_expert = jax.random.randint(key_star, (), 0, EXPERTS)
    expert_ids = jnp.arange(EXPERTS, dtype=jnp.int32)[None, :]
    hit = (expert_ids == star_expert) & (shard_ids == N_DP - 1)
    return jnp.where(hit, CAP, counts).astype(jnp.int32)


def plant(result, own_key, low, largest):
    longest = result.shape.index(max(result.shape))
    spots = []
    for shift in (0, 1):
        where = [jax.random.randint(jax.random.fold_in(own_key, axis), (), 0, length) for axis, length in enumerate(result.shape)]
        where[longest] = (where[longest] + shift) % result.shape[longest]
        spots.append(tuple(where))
    return result.at[spots[0]].set(low).at[spots[1]].set(largest)


def steps_of(own_key, dims, cuts, smallest, largest):
    def one(axis_at, shards_of):
        draws = jax.random.uniform(jax.random.fold_in(jax.random.fold_in(own_key, 6), axis_at), (shards_of,), jnp.float32, smallest / len(cuts), largest / len(cuts))
        return jnp.repeat(jnp.exp(draws), dims[axis_at] // shards_of).reshape((-1,) + (1,) * (len(dims) - axis_at - 1))

    level = one(*cuts[0])
    for cut in cuts[1:]:
        level = level * one(*cut)
    return level


def bell_draw(key, extent, scale, limit, shards=(), kind=jnp.bfloat16):
    drawn = scale * jax.random.normal(key, extent, jnp.float32)
    if shards:
        drawn = drawn * steps_of(key, extent, shards, -0.22, 0.18)
    return jnp.clip(drawn, -limit, limit).astype(kind)


def setup_inputs(seed: int = 0) -> dict:
    seeds = jax.random.split(jax.random.key(seed), 7)
    return {
        "saved_inputs": bell_draw(seeds[0], (N_DP, EXPERTS, CAP, D), 1.0, 6.0, ((0, 8), (1, 4))),
        "saved_grads": bell_draw(seeds[1], (N_DP, EXPERTS, CAP, FF), 1.0, 6.0, ((0, 8), (1, 4))),
        "row_counts": draw_row_counts(jax.random.fold_in(seeds[6], 71), 0),
        "row_seq": plant(jax.random.randint(seeds[3], (N_DP, EXPERTS, CAP), 0, SEQ_DEV), jax.random.fold_in(seeds[3], 1), 0, SEQ_DEV - 1).astype(jnp.int32),
        "proj_in": bell_draw(seeds[4], (D, K), D ** -0.5, 0.09375),
        "proj_out": bell_draw(seeds[5], (FF, K), FF ** -0.5, 0.15625),
    }


def shard_grads(shard_data, proj_in, proj_out):
    inputs, row_grads, counts, seq_ids = shard_data
    experts, capacity, width = inputs.shape
    in_proj = jnp.dot(inputs.reshape(experts * capacity, width), proj_in, preferred_element_type=jnp.float32)
    out_proj = jnp.dot(row_grads.reshape(experts * capacity, row_grads.shape[2]), proj_out, preferred_element_type=jnp.float32)
    proj_rank = in_proj.shape[1]
    outer_rows = (out_proj[:, :, None] * in_proj[:, None, :]).reshape(experts, capacity, proj_rank * proj_rank).astype(jnp.bfloat16)
    slot_ids = jnp.arange(capacity, dtype=jnp.int32)
    is_live = slot_ids[None, :] < counts[:, None]
    member = (seq_ids[:, None, :] == jnp.arange(SEQ_DEV, dtype=jnp.int32)[None, :, None]) & is_live[:, None, :]
    onehot = member.astype(jnp.bfloat16)
    summed = jnp.einsum("esc,eck->esk", onehot.astype(jnp.float32), outer_rows.astype(jnp.float32))
    return summed.astype(jnp.bfloat16)


def reference(saved_inputs, saved_grads, row_counts, row_seq, proj_in, proj_out):
    per_shard = lax.map(lambda shard_data: shard_grads(shard_data, proj_in, proj_out),
                        (saved_inputs, saved_grads, row_counts, row_seq))
    logged = jnp.transpose(per_shard, (1, 0, 2, 3)).reshape(EXPERTS, N_DP * SEQ_DEV, K * K)
    widened = logged.astype(jnp.float32)
    fisher = jnp.einsum("esi,esj->iej", widened, widened, precision=lax.Precision.HIGHEST)
    totals = jnp.sum(row_counts.astype(jnp.float32), axis=0)
    return logged, fisher / totals[None, :, None]
```

```python
import functools

import jax
import jax.numpy as jnp
from jax import lax
from jax.experimental import pallas as pl
from jax.experimental.pallas import tpu as pltpu
from jax.sharding import PartitionSpec as P

SEQ_DEV = 256
CHUNKS = 4
MESH = pl.DeviceIdType.MESH
NT = (((1,), (1,)), ((), ()))


def kernel(
    n_dp,
    n_exp,
    lo,
    count_ref,
    seq_ref,
    x_hbm,
    g_hbm,
    pin_hbm,
    pout_hbm,
    logged_ref,
    fisher_ref,
    xb,
    gb,
    pin,
    pout,
    fac,
    seqs,
    outer,
    onehot,
    gt,
    lg,
    in_sem,
    p_sem,
    send_sem,
    recv_sem,
    lsend_sem,
    lrecv_sem,
    local_sem,
):
    hi = n_dp // lo
    msgs = CHUNKS + 1
    rank = pin_hbm.shape[1]
    cap = x_hbm.shape[0]
    rows = cap // CHUNKS
    lanes = seq_ref.shape[1]
    share = SEQ_DEV // n_exp
    fb = fisher_ref.shape[0]

    dp = lax.axis_index("dp")
    ex = lax.axis_index("expert")
    z = dp // lo
    x = dp % lo

    p_copies = [
        pltpu.make_async_copy(pin_hbm, pin, p_sem.at[0]),
        pltpu.make_async_copy(pout_hbm, pout, p_sem.at[1]),
    ]
    for c in p_copies:
        c.start()

    def load(ch):
        at = pl.ds(ch * rows, rows)
        return (
            pltpu.make_async_copy(x_hbm.at[at], xb.at[at], in_sem.at[2 * ch]),
            pltpu.make_async_copy(g_hbm.at[at], gb.at[at], in_sem.at[2 * ch + 1]),
        )

    for ch in range(CHUNKS):
        for c in load(ch):
            c.start()

    barrier = pltpu.get_barrier_semaphore()

    def greet(device):
        pl.semaphore_signal(barrier, inc=1, device_id=device, device_id_type=MESH)

    for s in range(1, lo):
        greet((z * lo + lax.rem(x + s, lo), ex))
    for s in range(1, n_exp):
        greet((dp, lax.rem(ex + s, n_exp)))

    @pl.when(z > 0)
    def _():
        greet((dp - lo, ex))

    @pl.when(z < hi - 1)
    def _():
        greet((dp + lo, ex))

    def copy_of(blk, m, way, device):
        ref = seqs.at[blk] if m == 0 else fac.at[blk * CHUNKS + (m - 1)]
        return pltpu.make_async_remote_copy(
            src_ref=ref,
            dst_ref=ref,
            send_sem=send_sem.at[(way * hi + blk // lo) * msgs + m],
            recv_sem=recv_sem.at[blk * msgs + m],
            device_id=(device, ex),
            device_id_type=MESH,
        )

    def send_on(sz, m, act):
        blk = sz * lo + x

        @pl.when((sz <= z) & (z < hi - 1))
        def _():
            act(copy_of(blk, m, 0, dp + lo))

        @pl.when((sz >= z) & (z > 0))
        def _():
            act(copy_of(blk, m, 1, dp - lo))

        for s in range(1, lo):
            act(copy_of(blk, m, 1 + s, z * lo + lax.rem(x + s, lo)))

    start = lambda c: c.start()

    def recv(blk, m):
        copy_of(blk, m, 0, dp).wait_recv()

    slot = (
        lax.broadcasted_iota(jnp.int32, seq_ref.shape, 0) * lanes
        + lax.broadcasted_iota(jnp.int32, seq_ref.shape, 1)
    )
    seqs[dp] = jnp.where(slot < count_ref[0, 0], seq_ref[...], -1)

    for c in p_copies:
        c.wait()
    for ch in range(CHUNKS):
        for c in load(ch):
            c.wait()
        at = pl.ds(ch * rows, rows)
        a = jnp.dot(xb[at], pin[...], preferred_element_type=jnp.float32)
        b = jnp.dot(gb[at], pout[...], preferred_element_type=jnp.float32)
        both = jnp.concatenate([a, b, jnp.zeros((rows, 128 - 2 * rank), jnp.float32)], axis=1)
        fac[dp * CHUNKS + ch] = both.T[: 2 * rank].astype(jnp.bfloat16)
        if ch == 0:
            greeted = (lo - 1) + (n_exp - 1) + jnp.where(z > 0, 1, 0) + jnp.where(z < hi - 1, 1, 0)
            pl.semaphore_wait(barrier, greeted)
            send_on(z, 0, start)
        send_on(z, ch + 1, start)

    def build(blk):
        for ch in range(CHUNKS):
            at = pl.ds(ch * rows, rows)
            f = fac[blk * CHUNKS + ch].astype(jnp.float32)
            low = f[:rank]
            for k in range(rank):
                outer[k * rank : (k + 1) * rank, at] = (f[rank + k : rank + k + 1] * low).astype(
                    jnp.bfloat16
                )
        ids = seqs[blk]
        want = lax.broadcasted_iota(jnp.int32, (SEQ_DEV, lanes), 0)
        for c in range(cap // lanes):
            onehot[:, c * lanes : (c + 1) * lanes] = jnp.where(
                want == ids[c : c + 1], 1.0, 0.0
            ).astype(jnp.bfloat16)

    def gram():
        gt[...] = lax.dot_general(
            outer[...], onehot[...], NT, preferred_element_type=jnp.float32
        ).astype(jnp.bfloat16)
        mine = gt[pl.ds(pl.multiple_of(dp * fb, fb), fb), :]
        return lax.dot_general(mine, gt[...], NT, preferred_element_type=jnp.float32)

    build(dp)
    lg[...] = lax.dot_general(
        onehot[...], outer[...], NT, preferred_element_type=jnp.float32
    ).astype(jnp.bfloat16)

    def rows_of(e):
        return lg.at[pl.ds(pl.multiple_of(e * share, share), share)]

    def log_copy(s):
        to = lax.rem(ex + s, n_exp)
        return pltpu.make_async_remote_copy(
            src_ref=rows_of(to),
            dst_ref=logged_ref.at[ex],
            send_sem=lsend_sem.at[s - 1],
            recv_sem=lrecv_sem.at[s - 1],
            device_id=(dp, to),
            device_id_type=MESH,
        )

    for s in range(1, n_exp):
        log_copy(s).start()
    keep = pltpu.make_async_copy(rows_of(ex), logged_ref.at[ex], local_sem)
    keep.start()
    fisher_ref[...] = gram()

    def at_distance(d, carry):
        for m in range(msgs):
            for side in (-1, 1):
                sz = z + side * d

                @pl.when((sz >= 0) & (sz < hi))
                def _():
                    recv(sz * lo + x, m)
                    send_on(sz, m, start)

        def one(j, carry):
            col = lax.rem(j // 2 + 1, lo)
            dist = d - jnp.where(col > 0, 1, 0)
            side = lax.rem(j, 2)
            sz = z + dist * (2 * side - 1)

            @pl.when((sz >= 0) & (sz < hi) & ((dist > 0) | (side == 0)))
            def _():
                blk = sz * lo + lax.rem(x + col, lo)

                @pl.when(col > 0)
                def _():
                    for m in range(msgs):
                        recv(blk, m)

                build(blk)
                fisher_ref[...] += gram()

            return carry

        return lax.fori_loop(0, 2 * lo, one, carry)

    lax.fori_loop(1, hi + 1, at_distance, 0)

    live = jnp.zeros(seq_ref.shape, jnp.float32)
    for p in range(n_dp):
        live += jnp.where(seqs[p] >= 0, 1.0, 0.0)
    fisher_ref[...] = fisher_ref[...] / jnp.sum(live)

    def drain(sz, carry):
        for m in range(msgs):
            send_on(sz, m, lambda c: c.wait_send())
        return carry

    lax.fori_loop(0, hi, drain, 0)
    keep.wait()
    for s in range(1, n_exp):
        log_copy(s).wait()


def body(n_dp, n_exp, saved_inputs, saved_grads, row_counts, row_seq, proj_in, proj_out):
    cap, width = saved_inputs.shape[2:]
    ff = saved_grads.shape[3]
    rank = proj_in.shape[1]
    square = rank * rank
    lanes = 128
    lo = 2 if n_dp % 2 == 0 else 1
    hi = n_dp // lo
    share = SEQ_DEV // n_exp
    rows = cap // CHUNKS
    msgs = CHUNKS + 1
    vmem = pl.BlockSpec(memory_space=pltpu.VMEM)
    hbm = pl.BlockSpec(memory_space=pl.ANY)
    logged, fisher = pl.pallas_call(
        functools.partial(kernel, n_dp, n_exp, lo),
        out_shape=(
            jax.ShapeDtypeStruct((n_exp, share, square), jnp.bfloat16),
            jax.ShapeDtypeStruct((square // n_dp, square), jnp.float32),
        ),
        in_specs=[pl.BlockSpec(memory_space=pltpu.SMEM), vmem, hbm, hbm, hbm, hbm],
        out_specs=(hbm, vmem),
        scratch_shapes=[
            pltpu.VMEM((cap, width), jnp.bfloat16),
            pltpu.VMEM((cap, ff), jnp.bfloat16),
            pltpu.VMEM(proj_in.shape, jnp.bfloat16),
            pltpu.VMEM(proj_out.shape, jnp.bfloat16),
            pltpu.VMEM((n_dp * CHUNKS, 2 * rank, rows), jnp.bfloat16),
            pltpu.VMEM((n_dp, cap // lanes, lanes), jnp.int32),
            pltpu.VMEM((square, cap), jnp.bfloat16),
            pltpu.VMEM((SEQ_DEV, cap), jnp.bfloat16),
            pltpu.VMEM((square, SEQ_DEV), jnp.bfloat16),
            pltpu.VMEM((SEQ_DEV, square), jnp.bfloat16),
            pltpu.SemaphoreType.DMA((2 * CHUNKS,)),
            pltpu.SemaphoreType.DMA((2,)),
            pltpu.SemaphoreType.DMA(((lo + 1) * hi * msgs,)),
            pltpu.SemaphoreType.DMA((n_dp * msgs,)),
            pltpu.SemaphoreType.DMA((n_exp - 1,)),
            pltpu.SemaphoreType.DMA((n_exp - 1,)),
            pltpu.SemaphoreType.DMA,
        ],
        compiler_params=pltpu.CompilerParams(
            collective_id=0, has_side_effects=True, vmem_limit_bytes=56 * 1024 * 1024
        ),
    )(
        row_counts,
        row_seq.reshape(cap // lanes, lanes),
        saved_inputs.reshape(cap, width),
        saved_grads.reshape(cap, ff),
        proj_in,
        proj_out,
    )
    return logged, fisher.reshape(square // n_dp, 1, square)


def solution(mesh):
    in_specs = (
        P("dp", "expert", None, None),
        P("dp", "expert", None, None),
        P("dp", "expert"),
        P("dp", "expert", None),
        P(),
        P(),
    )
    out_specs = (P(None, ("dp", "expert"), None), P("dp", "expert", None))
    return jax.shard_map(
        functools.partial(body, mesh.shape["dp"], mesh.shape["expert"]),
        mesh=mesh,
        in_specs=in_specs,
        out_specs=out_specs,
        check_vma=False,
    )
```

```python
import functools

import jax
import jax.numpy as jnp
from jax import lax
from jax.experimental import pallas as pl
from jax.experimental.pallas import tpu as pltpu
from jax.sharding import PartitionSpec as P

SEQ_DEV = 256
CHUNKS = 4
MESH = pl.DeviceIdType.MESH
NT = (((1,), (1,)), ((), ()))


def kernel(
    n_dp,
    n_exp,
    lo,
    count_ref,
    seq_ref,
    x_hbm,
    g_hbm,
    pin_hbm,
    pout_hbm,
    logged_ref,
    fisher_ref,
    xb,
    gb,
    pin,
    pout,
    fac,
    seqs,
    outer,
    onehot,
    gt,
    lg,
    acc,
    in_sem,
    p_sem,
    send_sem,
    recv_sem,
    lsend_sem,
    lrecv_sem,
    local_sem,
):
    hi = n_dp // lo
    msgs = CHUNKS + 1
    rank = pin_hbm.shape[0]
    cap = x_hbm.shape[0]
    rows = cap // CHUNKS
    lanes = seq_ref.shape[1]
    share = SEQ_DEV // n_exp
    fb = acc.shape[0]

    dp = lax.axis_index("dp")
    ex = lax.axis_index("expert")
    z = dp // lo
    x = dp % lo

    p_copies = [
        pltpu.make_async_copy(pin_hbm, pin, p_sem.at[0]),
        pltpu.make_async_copy(pout_hbm, pout, p_sem.at[1]),
    ]
    for c in p_copies:
        c.start()

    def load(ch):
        at = pl.ds(ch * rows, rows)
        return (
            pltpu.make_async_copy(x_hbm.at[at], xb.at[at], in_sem.at[2 * ch]),
            pltpu.make_async_copy(g_hbm.at[at], gb.at[at], in_sem.at[2 * ch + 1]),
        )

    for ch in range(CHUNKS):
        for c in load(ch):
            c.start()

    barrier = pltpu.get_barrier_semaphore()

    def greet(device):
        pl.semaphore_signal(barrier, inc=1, device_id=device, device_id_type=MESH)

    for s in range(1, lo):
        greet((z * lo + lax.rem(x + s, lo), ex))
    for s in range(1, n_exp):
        greet((dp, lax.rem(ex + s, n_exp)))

    @pl.when(z > 0)
    def _():
        greet((dp - lo, ex))

    @pl.when(z < hi - 1)
    def _():
        greet((dp + lo, ex))

    def copy_of(blk, m, way, device):
        ref = seqs.at[blk] if m == 0 else fac.at[blk * CHUNKS + (m - 1)]
        return pltpu.make_async_remote_copy(
            src_ref=ref,
            dst_ref=ref,
            send_sem=send_sem.at[(way * hi + blk // lo) * msgs + m],
            recv_sem=recv_sem.at[blk * msgs + m],
            device_id=(device, ex),
            device_id_type=MESH,
        )

    def send_on(sz, m, act):
        blk = sz * lo + x

        @pl.when((sz <= z) & (z < hi - 1))
        def _():
            act(copy_of(blk, m, 0, dp + lo))

        @pl.when((sz >= z) & (z > 0))
        def _():
            act(copy_of(blk, m, 1, dp - lo))

        for s in range(1, lo):
            act(copy_of(blk, m, 1 + s, z * lo + lax.rem(x + s, lo)))

    start = lambda c: c.start()

    def recv(blk, m):
        copy_of(blk, m, 0, dp).wait_recv()

    slot = (
        lax.broadcasted_iota(jnp.int32, seq_ref.shape, 0) * lanes
        + lax.broadcasted_iota(jnp.int32, seq_ref.shape, 1)
    )
    seqs[dp] = jnp.where(slot < count_ref[0, 0], seq_ref[...], -1)

    for c in p_copies:
        c.wait()
    for ch in range(CHUNKS):
        for c in load(ch):
            c.wait()
        at = pl.ds(ch * rows, rows)
        a = lax.dot_general(xb[at], pin[...], NT, preferred_element_type=jnp.float32)
        b = lax.dot_general(gb[at], pout[...], NT, preferred_element_type=jnp.float32)
        both = jnp.concatenate([a, b, jnp.zeros((rows, 128 - 2 * rank), jnp.float32)], axis=1)
        fac[dp * CHUNKS + ch] = both.T[: 2 * rank].astype(jnp.bfloat16)
        if ch == 0:
            greeted = (lo - 1) + (n_exp - 1) + jnp.where(z > 0, 1, 0) + jnp.where(z < hi - 1, 1, 0)
            pl.semaphore_wait(barrier, greeted)
            send_on(z, 0, start)
        send_on(z, ch + 1, start)

    def build(blk):
        for ch in range(CHUNKS):
            at = pl.ds(ch * rows, rows)
            f = fac[blk * CHUNKS + ch]
            wide = f[rank:].astype(jnp.float32)
            for k in range(rank):
                row = jnp.broadcast_to(wide[k : k + 1], (16, rows)).astype(jnp.bfloat16)
                for h in range(0, rank, 16):
                    outer[k * rank + h : k * rank + h + 16, at] = row * f[h : h + 16]
        ids = seqs[blk]
        want = lax.broadcasted_iota(jnp.int32, (SEQ_DEV, lanes), 0)
        for c in range(cap // lanes):
            onehot[:, c * lanes : (c + 1) * lanes] = jnp.where(
                want == ids[c : c + 1], 1.0, 0.0
            ).astype(jnp.bfloat16)

    def gram():
        gt[...] = lax.dot_general(
            outer[...], onehot[...], NT, preferred_element_type=jnp.float32
        ).astype(jnp.bfloat16)
        mine = gt[pl.ds(pl.multiple_of(dp * fb, fb), fb), :]
        return lax.dot_general(mine, gt[...], NT, preferred_element_type=jnp.float32)

    build(dp)
    lg[...] = lax.dot_general(
        onehot[...], outer[...], NT, preferred_element_type=jnp.float32
    ).astype(jnp.bfloat16)

    def rows_of(e):
        return lg.at[pl.ds(pl.multiple_of(e * share, share), share)]

    def log_copy(s):
        to = lax.rem(ex + s, n_exp)
        return pltpu.make_async_remote_copy(
            src_ref=rows_of(to),
            dst_ref=logged_ref.at[ex],
            send_sem=lsend_sem.at[s - 1],
            recv_sem=lrecv_sem.at[s - 1],
            device_id=(dp, to),
            device_id_type=MESH,
        )

    def receive(d):
        for m in range(msgs):
            for side in (-1, 1):
                sz = z + side * d

                @pl.when((sz >= 0) & (sz < hi))
                def _():
                    recv(sz * lo + x, m)
                    send_on(sz, m, start)

    for s in range(1, n_exp):
        log_copy(s).start()
    keep = pltpu.make_async_copy(rows_of(ex), logged_ref.at[ex], local_sem)
    keep.start()
    receive(1)
    acc[...] = gram()

    def at_distance(d, carry):
        receive(d + 1)

        def one(j, carry):
            col = lax.rem(j // 2 + 1, lo)
            dist = d - jnp.where(col > 0, 1, 0)
            side = lax.rem(j, 2)
            sz = z + dist * (2 * side - 1)

            @pl.when((sz >= 0) & (sz < hi) & ((dist > 0) | (side == 0)))
            def _():
                blk = sz * lo + lax.rem(x + col, lo)

                @pl.when(col > 0)
                def _():
                    for m in range(msgs):
                        recv(blk, m)

                build(blk)
                acc[...] += gram()

            return carry

        return lax.fori_loop(0, 2 * lo, one, carry)

    lax.fori_loop(1, hi + 1, at_distance, 0)

    live = jnp.zeros(seq_ref.shape, jnp.float32)
    for p in range(n_dp):
        live += jnp.where(seqs[p] >= 0, 1.0, 0.0)
    scale = 1.0 / jnp.sum(live)
    tiles = acc.shape[1] // lanes
    for c in range(tiles):
        fisher_ref[pl.ds(c, fb, stride=tiles), :] = acc[:, c * lanes : (c + 1) * lanes] * scale

    def drain(sz, carry):
        for m in range(msgs):
            send_on(sz, m, lambda c: c.wait_send())
        return carry

    lax.fori_loop(0, hi, drain, 0)
    keep.wait()
    for s in range(1, n_exp):
        log_copy(s).wait()


def place_kernel(pieces, *refs):
    sems = refs[-1]
    half = (len(refs) - 1) // 2
    copies = []
    for src, dst in zip(refs[:half], refs[half:-1]):
        step = src.shape[0] // pieces
        for i in range(pieces):
            at = pl.ds(i * step, step)
            copies.append(pltpu.make_async_copy(src.at[at], dst.at[at], sems.at[len(copies)]))
    for c in copies:
        c.start()
    for c in copies:
        c.wait()


def place(*arrays):
    pieces = 4
    hbm = pl.BlockSpec(memory_space=pl.ANY)
    return pl.pallas_call(
        functools.partial(place_kernel, pieces),
        out_shape=tuple(jax.ShapeDtypeStruct(a.shape, a.dtype) for a in arrays),
        in_specs=[hbm] * len(arrays),
        out_specs=(hbm,) * len(arrays),
        scratch_shapes=[pltpu.SemaphoreType.DMA((pieces * len(arrays),))],
        compiler_params=pltpu.CompilerParams(vmem_limit_bytes=60 * 1024 * 1024),
        name="place",
    )(*arrays)


def body(n_dp, n_exp, saved_inputs, saved_grads, row_counts, row_seq, proj_in, proj_out):
    cap, width = saved_inputs.shape[2:]
    ff = saved_grads.shape[3]
    rank = proj_in.shape[1]
    square = rank * rank
    lanes = 128
    lo = 2 if n_dp % 2 == 0 else 1
    hi = n_dp // lo
    share = SEQ_DEV // n_exp
    rows = cap // CHUNKS
    msgs = CHUNKS + 1
    vmem = pl.BlockSpec(memory_space=pltpu.VMEM)
    hbm = pl.BlockSpec(memory_space=pl.ANY)
    logged, fisher = pl.pallas_call(
        functools.partial(kernel, n_dp, n_exp, lo),
        out_shape=(
            jax.ShapeDtypeStruct((n_exp, share, square), jnp.bfloat16),
            jax.ShapeDtypeStruct((square // n_dp * square // lanes, lanes), jnp.float32),
        ),
        in_specs=[pl.BlockSpec(memory_space=pltpu.SMEM), vmem, hbm, hbm, hbm, hbm],
        out_specs=(hbm, vmem),
        scratch_shapes=[
            pltpu.VMEM((cap, width), jnp.bfloat16),
            pltpu.VMEM((cap, ff), jnp.bfloat16),
            pltpu.VMEM((rank, width), jnp.bfloat16),
            pltpu.VMEM((rank, ff), jnp.bfloat16),
            pltpu.VMEM((n_dp * CHUNKS, 2 * rank, rows), jnp.bfloat16),
            pltpu.VMEM((n_dp, cap // lanes, lanes), jnp.int32),
            pltpu.VMEM((square, cap), jnp.bfloat16),
            pltpu.VMEM((SEQ_DEV, cap), jnp.bfloat16),
            pltpu.VMEM((square, SEQ_DEV), jnp.bfloat16),
            pltpu.VMEM((SEQ_DEV, square), jnp.bfloat16),
            pltpu.VMEM((square // n_dp, square), jnp.float32),
            pltpu.SemaphoreType.DMA((2 * CHUNKS,)),
            pltpu.SemaphoreType.DMA((2,)),
            pltpu.SemaphoreType.DMA(((lo + 1) * hi * msgs,)),
            pltpu.SemaphoreType.DMA((n_dp * msgs,)),
            pltpu.SemaphoreType.DMA((n_exp - 1,)),
            pltpu.SemaphoreType.DMA((n_exp - 1,)),
            pltpu.SemaphoreType.DMA,
        ],
        compiler_params=pltpu.CompilerParams(
            collective_id=0, has_side_effects=True, vmem_limit_bytes=56 * 1024 * 1024
        ),
    )(
        row_counts,
        row_seq.reshape(cap // lanes, lanes),
        saved_inputs.reshape(cap, width),
        saved_grads.reshape(cap, ff),
        proj_in.T,
        proj_out.T,
    )
    logged, fisher = place(logged, fisher)
    return logged, fisher.reshape(square // n_dp, 1, square)


def solution(mesh):
    in_specs = (
        P("dp", "expert", None, None),
        P("dp", "expert", None, None),
        P("dp", "expert"),
        P("dp", "expert", None),
        P(),
        P(),
    )
    out_specs = (P(None, ("dp", "expert"), None), P("dp", "expert", None))
    return jax.shard_map(
        functools.partial(body, mesh.shape["dp"], mesh.shape["expert"]),
        mesh=mesh,
        in_specs=in_specs,
        out_specs=out_specs,
        check_vma=False,
    )
```

```python
import functools

import jax
import jax.numpy as jnp
from jax import lax
from jax.experimental import pallas as pl
from jax.experimental.pallas import tpu as pltpu
from jax.sharding import PartitionSpec as P

SEQ_DEV = 256
CHUNKS = 4
PIECES = 2
MESH = pl.DeviceIdType.MESH
NT = (((1,), (1,)), ((), ()))


def kernel(
    n_dp,
    n_exp,
    lo,
    count_ref,
    seq_ref,
    x_hbm,
    g_hbm,
    pin_hbm,
    pout_hbm,
    logged_ref,
    fisher_ref,
    xb,
    gb,
    pin,
    pout,
    wide_in,
    wide_out,
    fac,
    seqs,
    outer,
    onehot,
    gt,
    lg,
    acc,
    give,
    got,
    lives,
    in_sem,
    p_sem,
    send_sem,
    recv_sem,
    lsend_sem,
    lrecv_sem,
    xsend_sem,
    xrecv_sem,
    local_sem,
):
    hi = n_dp // lo
    msgs = CHUNKS + 1
    rank = pin_hbm.shape[0]
    cap = x_hbm.shape[0]
    rows = cap // CHUNKS
    lanes = seq_ref.shape[1]
    share = SEQ_DEV // n_exp
    fb = acc.shape[0] // lo

    dp = lax.axis_index("dp")
    ex = lax.axis_index("expert")
    z = dp // lo
    x = dp % lo

    p_copies = [
        pltpu.make_async_copy(pin_hbm, pin, p_sem.at[0]),
        pltpu.make_async_copy(pout_hbm, pout, p_sem.at[1]),
    ]
    for c in p_copies:
        c.start()

    def load(ch):
        at = pl.ds(ch * rows, rows)
        return (
            pltpu.make_async_copy(x_hbm.at[at], xb.at[at], in_sem.at[2 * ch]),
            pltpu.make_async_copy(g_hbm.at[at], gb.at[at], in_sem.at[2 * ch + 1]),
        )

    for ch in range(CHUNKS):
        for c in load(ch):
            c.start()

    barrier = pltpu.get_barrier_semaphore()

    def greet(device):
        pl.semaphore_signal(barrier, inc=1, device_id=device, device_id_type=MESH)

    for s in range(1, lo):
        greet((z * lo + lax.rem(x + s, lo), ex))
    for s in range(1, n_exp):
        greet((dp, lax.rem(ex + s, n_exp)))

    @pl.when(z > 0)
    def _():
        greet((dp - lo, ex))

    @pl.when(z < hi - 1)
    def _():
        greet((dp + lo, ex))

    def copy_of(blk, m, way, device):
        ref = seqs.at[blk] if m == 0 else fac.at[blk * CHUNKS + (m - 1)]
        return pltpu.make_async_remote_copy(
            src_ref=ref,
            dst_ref=ref,
            send_sem=send_sem.at[(way * hi + blk) * msgs + m],
            recv_sem=recv_sem.at[blk * msgs + m],
            device_id=(device, ex),
            device_id_type=MESH,
        )

    def send_on(sz, m, act):
        @pl.when((sz <= z) & (z < hi - 1))
        def _():
            act(copy_of(sz, m, 0, dp + lo))

        @pl.when((sz >= z) & (z > 0))
        def _():
            act(copy_of(sz, m, 1, dp - lo))

    start = lambda c: c.start()

    def recv(blk, m):
        copy_of(blk, m, 0, dp).wait_recv()

    slot = (
        lax.broadcasted_iota(jnp.int32, seq_ref.shape, 0) * lanes
        + lax.broadcasted_iota(jnp.int32, seq_ref.shape, 1)
    )
    seqs[z] = jnp.where(slot < count_ref[0, 0], seq_ref[...], -1)

    for c in p_copies:
        c.wait()
    for src, dst, before in ((pin, wide_in, 0), (pout, wide_out, rank)):
        blank = lambda r: [jnp.zeros((r, src.shape[1]), jnp.float32)] if r else []
        tall = blank(before) + [src[...].astype(jnp.float32)] + blank(lanes - rank - before)
        dst[...] = jnp.concatenate(tall, axis=0).T.astype(jnp.bfloat16)
    for ch in range(CHUNKS):
        for c in load(ch):
            c.wait()
        at = pl.ds(ch * rows, rows)
        both = jnp.dot(xb[at], wide_in[...], preferred_element_type=jnp.float32)
        both += jnp.dot(gb[at], wide_out[...], preferred_element_type=jnp.float32)
        fac[z * CHUNKS + ch] = both.T[: 2 * rank].astype(jnp.bfloat16)
        if ch == 0:
            greeted = (lo - 1) + (n_exp - 1) + jnp.where(z > 0, 1, 0) + jnp.where(z < hi - 1, 1, 0)
            pl.semaphore_wait(barrier, greeted)
            send_on(z, 0, start)
        send_on(z, ch + 1, start)

    def build(blk):
        for ch in range(CHUNKS):
            at = pl.ds(ch * rows, rows)
            f = fac[blk * CHUNKS + ch]
            wide = f[rank:].astype(jnp.float32)
            for k in range(rank):
                row = jnp.broadcast_to(wide[k : k + 1], (16, rows)).astype(jnp.bfloat16)
                for h in range(0, rank, 16):
                    outer[k * rank + h : k * rank + h + 16, at] = row * f[h : h + 16]
        ids = seqs[blk]
        want = lax.broadcasted_iota(jnp.int32, (SEQ_DEV, lanes), 0)
        for c in range(cap // lanes):
            onehot[:, c * lanes : (c + 1) * lanes] = jnp.where(
                want == ids[c : c + 1], 1.0, 0.0
            ).astype(jnp.bfloat16)

    def gram():
        gt[...] = lax.dot_general(
            outer[...], onehot[...], NT, preferred_element_type=jnp.float32
        ).astype(jnp.bfloat16)
        mine = gt[pl.ds(pl.multiple_of(z * lo * fb, lo * fb), lo * fb), :]
        return lax.dot_general(mine, gt[...], NT, preferred_element_type=jnp.float32)

    build(z)
    lg[...] = lax.dot_general(
        onehot[...], outer[...], NT, preferred_element_type=jnp.float32
    ).astype(jnp.bfloat16)

    def rows_of(e):
        return lg.at[pl.ds(pl.multiple_of(e * share, share), share)]

    def log_copy(s):
        to = lax.rem(ex + s, n_exp)
        return pltpu.make_async_remote_copy(
            src_ref=rows_of(to),
            dst_ref=logged_ref.at[ex],
            send_sem=lsend_sem.at[s - 1],
            recv_sem=lrecv_sem.at[s - 1],
            device_id=(dp, to),
            device_id_type=MESH,
        )

    def receive(d):
        for m in range(msgs):
            for side in (-1, 1):
                sz = z + side * d

                @pl.when((sz >= 0) & (sz < hi))
                def _():
                    recv(sz, m)
                    send_on(sz, m, start)

    for s in range(1, n_exp):
        log_copy(s).start()
    keep = pltpu.make_async_copy(rows_of(ex), logged_ref.at[ex], local_sem)
    keep.start()
    receive(1)
    acc[...] = gram()

    def at_distance(d, carry):
        receive(d + 1)

        def one(side, carry):
            sz = z + d * (2 * side - 1)

            @pl.when((sz >= 0) & (sz < hi))
            def _():
                build(sz)
                acc[...] += gram()

            return carry

        return lax.fori_loop(0, 2, one, carry)

    lax.fori_loop(1, hi, at_distance, 0)

    live = jnp.zeros(seq_ref.shape, jnp.float32)
    for p in range(hi):
        live += jnp.where(seqs[p] >= 0, 1.0, 0.0)
    lives[0] = live

    piece = fb // PIECES

    def rows_at(q):
        return pl.ds(q * piece, piece)

    def across(s, q):
        to = z * lo + lax.rem(x + s, lo)
        k = (s - 1) * (PIECES + 1) + q + 1
        src, dst = (lives.at[0], lives.at[s]) if q < 0 else (
            give.at[s, rows_at(q)],
            got.at[s, rows_at(q)],
        )
        return pltpu.make_async_remote_copy(
            src_ref=src,
            dst_ref=dst,
            send_sem=xsend_sem.at[k],
            recv_sem=xrecv_sem.at[k],
            device_id=(to, ex),
            device_id_type=MESH,
        )

    for s in range(1, lo):
        across(s, -1).start()
        theirs = lax.rem(x + s, lo) * fb
        for q in range(PIECES):
            at = pl.ds(pl.multiple_of(theirs + q * piece, piece), piece)
            give[s, rows_at(q)] = acc[at].astype(jnp.bfloat16)
            across(s, q).start()
    for s in range(1, lo):
        across(s, -1).wait_recv()
        live += lives[s]
    scale = 1.0 / jnp.sum(live)
    tiles = acc.shape[1] // lanes
    for q in range(PIECES):
        at = pl.ds(pl.multiple_of(x * fb + q * piece, piece), piece)
        total = acc[at]
        for s in range(1, lo):
            across(s, q).wait_recv()
            total += got[s, rows_at(q)].astype(jnp.float32)
        total *= scale
        for c in range(tiles):
            fisher_ref[pl.ds(q * piece * tiles + c, piece, stride=tiles), :] = total[
                :, c * lanes : (c + 1) * lanes
            ]

    def drain(sz, carry):
        for m in range(msgs):
            send_on(sz, m, lambda c: c.wait_send())
        return carry

    lax.fori_loop(0, hi, drain, 0)
    for s in range(1, lo):
        for q in range(-1, PIECES):
            across(s, q).wait_send()
    keep.wait()
    for s in range(1, n_exp):
        log_copy(s).wait()


def place_kernel(pieces, *refs):
    in_sems, out_sems = refs[-2:]
    n = (len(refs) - 2) // 3
    loads, stores = [], []
    for src, dst, held in zip(refs[:n], refs[n : 2 * n], refs[2 * n : 3 * n]):
        step = src.shape[0] // pieces
        for i in range(pieces):
            at = pl.ds(i * step, step)
            k = len(loads)
            loads.append(pltpu.make_async_copy(src.at[at], held.at[at], in_sems.at[k]))
            stores.append(pltpu.make_async_copy(held.at[at], dst.at[at], out_sems.at[k]))
    for c in loads:
        c.start()
    for c, d in zip(loads, stores):
        c.wait()
        d.start()
    for d in stores:
        d.wait()


def place(*arrays):
    pieces = 4
    hbm = pl.BlockSpec(memory_space=pl.ANY)
    return pl.pallas_call(
        functools.partial(place_kernel, pieces),
        out_shape=tuple(jax.ShapeDtypeStruct(a.shape, a.dtype) for a in arrays),
        in_specs=[hbm] * len(arrays),
        out_specs=(hbm,) * len(arrays),
        scratch_shapes=[pltpu.VMEM(a.shape, a.dtype) for a in arrays]
        + [pltpu.SemaphoreType.DMA((pieces * len(arrays),))] * 2,
        compiler_params=pltpu.CompilerParams(vmem_limit_bytes=60 * 1024 * 1024),
        name="place",
    )(*arrays)


def body(n_dp, n_exp, saved_inputs, saved_grads, row_counts, row_seq, proj_in, proj_out):
    cap, width = saved_inputs.shape[2:]
    ff = saved_grads.shape[3]
    rank = proj_in.shape[1]
    square = rank * rank
    lanes = 128
    lo = 2 if n_dp % 2 == 0 else 1
    hi = n_dp // lo
    share = SEQ_DEV // n_exp
    rows = cap // CHUNKS
    msgs = CHUNKS + 1
    vmem = pl.BlockSpec(memory_space=pltpu.VMEM)
    hbm = pl.BlockSpec(memory_space=pl.ANY)
    logged, fisher = pl.pallas_call(
        functools.partial(kernel, n_dp, n_exp, lo),
        out_shape=(
            jax.ShapeDtypeStruct((n_exp, share, square), jnp.bfloat16),
            jax.ShapeDtypeStruct((square // n_dp * square // lanes, lanes), jnp.float32),
        ),
        in_specs=[pl.BlockSpec(memory_space=pltpu.SMEM), vmem, hbm, hbm, hbm, hbm],
        out_specs=(hbm, vmem),
        scratch_shapes=[
            pltpu.VMEM((cap, width), jnp.bfloat16),
            pltpu.VMEM((cap, ff), jnp.bfloat16),
            pltpu.VMEM((rank, width), jnp.bfloat16),
            pltpu.VMEM((rank, ff), jnp.bfloat16),
            pltpu.VMEM((width, lanes), jnp.bfloat16),
            pltpu.VMEM((ff, lanes), jnp.bfloat16),
            pltpu.VMEM((hi * CHUNKS, 2 * rank, rows), jnp.bfloat16),
            pltpu.VMEM((hi, cap // lanes, lanes), jnp.int32),
            pltpu.VMEM((square, cap), jnp.bfloat16),
            pltpu.VMEM((SEQ_DEV, cap), jnp.bfloat16),
            pltpu.VMEM((square, SEQ_DEV), jnp.bfloat16),
            pltpu.VMEM((SEQ_DEV, square), jnp.bfloat16),
            pltpu.VMEM((square // hi, square), jnp.float32),
            pltpu.VMEM((lo, square // n_dp, square), jnp.bfloat16),
            pltpu.VMEM((lo, square // n_dp, square), jnp.bfloat16),
            pltpu.VMEM((lo, cap // lanes, lanes), jnp.float32),
            pltpu.SemaphoreType.DMA((2 * CHUNKS,)),
            pltpu.SemaphoreType.DMA((2,)),
            pltpu.SemaphoreType.DMA((2 * hi * msgs,)),
            pltpu.SemaphoreType.DMA((hi * msgs,)),
            pltpu.SemaphoreType.DMA((n_exp - 1,)),
            pltpu.SemaphoreType.DMA((n_exp - 1,)),
            pltpu.SemaphoreType.DMA((max(lo - 1, 1) * (PIECES + 1),)),
            pltpu.SemaphoreType.DMA((max(lo - 1, 1) * (PIECES + 1),)),
            pltpu.SemaphoreType.DMA,
        ],
        compiler_params=pltpu.CompilerParams(
            collective_id=0, has_side_effects=True, vmem_limit_bytes=56 * 1024 * 1024
        ),
    )(
        row_counts,
        row_seq.reshape(cap // lanes, lanes),
        saved_inputs.reshape(cap, width),
        saved_grads.reshape(cap, ff),
        proj_in.T,
        proj_out.T,
    )
    logged, fisher = place(logged, fisher)
    return logged, fisher.reshape(square // n_dp, 1, square)


def solution(mesh):
    in_specs = (
        P("dp", "expert", None, None),
        P("dp", "expert", None, None),
        P("dp", "expert"),
        P("dp", "expert", None),
        P(),
        P(),
    )
    out_specs = (P(None, ("dp", "expert"), None), P("dp", "expert", None))
    return jax.shard_map(
        functools.partial(body, mesh.shape["dp"], mesh.shape["expert"]),
        mesh=mesh,
        in_specs=in_specs,
        out_specs=out_specs,
        check_vma=False,
    )
```

```python
import functools

import jax
import jax.numpy as jnp
from jax import lax
from jax.experimental import pallas as pl
from jax.experimental.pallas import tpu as pltpu
from jax.sharding import PartitionSpec as P

SEQ_DEV = 256
CHUNKS = 4
AHEAD = 2
PIECES = 2
MESH = pl.DeviceIdType.MESH
NT = (((1,), (1,)), ((), ()))


def kernel(
    n_dp,
    n_exp,
    lo,
    count_ref,
    seq_ref,
    x_hbm,
    g_hbm,
    pin_hbm,
    pout_hbm,
    logged_ref,
    fisher_ref,
    xb,
    gb,
    pin,
    pout,
    wide_in,
    wide_out,
    fac,
    seqs,
    outer,
    onehot,
    gt,
    lg,
    acc,
    give,
    got,
    lives,
    in_sem,
    p_sem,
    send_sem,
    recv_sem,
    lsend_sem,
    lrecv_sem,
    xsend_sem,
    xrecv_sem,
    local_sem,
):
    hi = n_dp // lo
    msgs = CHUNKS + 1
    rank = pin_hbm.shape[0]
    cap = x_hbm.shape[0]
    rows = cap // CHUNKS
    lanes = seq_ref.shape[1]
    share = SEQ_DEV // n_exp
    fb = acc.shape[0] // lo

    dp = lax.axis_index("dp")
    ex = lax.axis_index("expert")
    z = dp // lo
    x = dp % lo

    p_copies = [
        pltpu.make_async_copy(pin_hbm, pin, p_sem.at[0]),
        pltpu.make_async_copy(pout_hbm, pout, p_sem.at[1]),
    ]
    for c in p_copies:
        c.start()

    def load(ch):
        at = pl.ds(ch * rows, rows)
        return (
            pltpu.make_async_copy(x_hbm.at[at], xb.at[at], in_sem.at[2 * ch]),
            pltpu.make_async_copy(g_hbm.at[at], gb.at[at], in_sem.at[2 * ch + 1]),
        )

    for ch in range(AHEAD):
        for c in load(ch):
            c.start()

    barrier = pltpu.get_barrier_semaphore()

    def greet(device):
        pl.semaphore_signal(barrier, inc=1, device_id=device, device_id_type=MESH)

    for s in range(1, lo):
        greet((z * lo + lax.rem(x + s, lo), ex))
    for s in range(1, n_exp):
        greet((dp, lax.rem(ex + s, n_exp)))

    for s in range(1, hi):
        greet((lax.rem(z + s, hi) * lo + x, ex))

    def copy_of(src, m, s):
        ref = seqs.at[src] if m == 0 else fac.at[src * CHUNKS + (m - 1)]
        return pltpu.make_async_remote_copy(
            src_ref=ref,
            dst_ref=ref,
            send_sem=send_sem.at[(s - 1) * msgs + m],
            recv_sem=recv_sem.at[src * msgs + m],
            device_id=(lax.rem(z + s, hi) * lo + x, ex),
            device_id_type=MESH,
        )

    def send(m):
        for s in range(1, hi):
            copy_of(z, m, s).start()

    slot = (
        lax.broadcasted_iota(jnp.int32, seq_ref.shape, 0) * lanes
        + lax.broadcasted_iota(jnp.int32, seq_ref.shape, 1)
    )
    seqs[z] = jnp.where(slot < count_ref[0, 0], seq_ref[...], -1)

    for c in p_copies:
        c.wait()
    for src, dst, before in ((pin, wide_in, 0), (pout, wide_out, rank)):
        blank = lambda r: [jnp.zeros((r, src.shape[1]), jnp.float32)] if r else []
        tall = blank(before) + [src[...].astype(jnp.float32)] + blank(lanes - rank - before)
        dst[...] = jnp.concatenate(tall, axis=0).T.astype(jnp.bfloat16)
    for ch in range(CHUNKS):
        for c in load(ch):
            c.wait()
        if ch + AHEAD < CHUNKS:
            for c in load(ch + AHEAD):
                c.start()
        at = pl.ds(ch * rows, rows)
        both = jnp.dot(xb[at], wide_in[...], preferred_element_type=jnp.float32)
        both += jnp.dot(gb[at], wide_out[...], preferred_element_type=jnp.float32)
        fac[z * CHUNKS + ch] = both.T[: 2 * rank].astype(jnp.bfloat16)
        if ch == 0:
            pl.semaphore_wait(barrier, (lo - 1) + (n_exp - 1) + (hi - 1))
            send(0)
        send(ch + 1)

    def build(blk):
        for ch in range(CHUNKS):
            at = pl.ds(ch * rows, rows)
            f = fac[blk * CHUNKS + ch]
            wide = f[rank:].astype(jnp.float32)
            for k in range(rank):
                row = jnp.broadcast_to(wide[k : k + 1], (16, rows)).astype(jnp.bfloat16)
                for h in range(0, rank, 16):
                    outer[k * rank + h : k * rank + h + 16, at] = row * f[h : h + 16]
        ids = seqs[blk]
        want = lax.broadcasted_iota(jnp.int32, (SEQ_DEV, lanes), 0)
        for c in range(cap // lanes):
            onehot[:, c * lanes : (c + 1) * lanes] = jnp.where(
                want == ids[c : c + 1], 1.0, 0.0
            ).astype(jnp.bfloat16)

    def gram():
        gt[...] = lax.dot_general(
            outer[...], onehot[...], NT, preferred_element_type=jnp.float32
        ).astype(jnp.bfloat16)
        mine = gt[pl.ds(pl.multiple_of(z * lo * fb, lo * fb), lo * fb), :]
        return lax.dot_general(mine, gt[...], NT, preferred_element_type=jnp.float32)

    build(z)
    lg[...] = lax.dot_general(
        onehot[...], outer[...], NT, preferred_element_type=jnp.float32
    ).astype(jnp.bfloat16)

    def rows_of(e):
        return lg.at[pl.ds(pl.multiple_of(e * share, share), share)]

    def log_copy(s):
        to = lax.rem(ex + s, n_exp)
        return pltpu.make_async_remote_copy(
            src_ref=rows_of(to),
            dst_ref=logged_ref.at[ex],
            send_sem=lsend_sem.at[s - 1],
            recv_sem=lrecv_sem.at[s - 1],
            device_id=(dp, to),
            device_id_type=MESH,
        )

    for s in range(1, n_exp):
        log_copy(s).start()
    keep = pltpu.make_async_copy(rows_of(ex), logged_ref.at[ex], local_sem)
    keep.start()
    acc[...] = gram()

    def at_distance(d, carry):
        def one(side, carry):
            sz = z + d * (2 * side - 1)

            @pl.when((sz >= 0) & (sz < hi))
            def _():
                for m in range(msgs):
                    copy_of(sz, m, 1).wait_recv()
                build(sz)
                acc[...] += gram()

            return carry

        return lax.fori_loop(0, 2, one, carry)

    lax.fori_loop(1, hi, at_distance, 0)

    live = jnp.zeros(seq_ref.shape, jnp.float32)
    for p in range(hi):
        live += jnp.where(seqs[p] >= 0, 1.0, 0.0)
    lives[0] = live

    piece = fb // PIECES

    def rows_at(q):
        return pl.ds(q * piece, piece)

    def across(s, q):
        to = z * lo + lax.rem(x + s, lo)
        k = (s - 1) * (PIECES + 1) + q + 1
        src, dst = (lives.at[0], lives.at[s]) if q < 0 else (
            give.at[s, rows_at(q)],
            got.at[s, rows_at(q)],
        )
        return pltpu.make_async_remote_copy(
            src_ref=src,
            dst_ref=dst,
            send_sem=xsend_sem.at[k],
            recv_sem=xrecv_sem.at[k],
            device_id=(to, ex),
            device_id_type=MESH,
        )

    for s in range(1, lo):
        across(s, -1).start()
        theirs = lax.rem(x + s, lo) * fb
        for q in range(PIECES):
            at = pl.ds(pl.multiple_of(theirs + q * piece, piece), piece)
            give[s, rows_at(q)] = acc[at].astype(jnp.bfloat16)
            across(s, q).start()
    for s in range(1, lo):
        across(s, -1).wait_recv()
        live += lives[s]
    scale = 1.0 / jnp.sum(live)
    tiles = acc.shape[1] // lanes
    for q in range(PIECES):
        at = pl.ds(pl.multiple_of(x * fb + q * piece, piece), piece)
        total = acc[at]
        for s in range(1, lo):
            across(s, q).wait_recv()
            total += got[s, rows_at(q)].astype(jnp.float32)
        total *= scale
        for c in range(tiles):
            fisher_ref[pl.ds(q * piece * tiles + c, piece, stride=tiles), :] = total[
                :, c * lanes : (c + 1) * lanes
            ]

    for s in range(1, hi):
        for m in range(msgs):
            copy_of(z, m, s).wait_send()
    for s in range(1, lo):
        for q in range(-1, PIECES):
            across(s, q).wait_send()
    keep.wait()
    for s in range(1, n_exp):
        log_copy(s).wait()


def place_kernel(pieces, *refs):
    sems = refs[-1]
    n = len(refs) // 2
    stores = []
    for src, dst in zip(refs[:n], refs[n:-1]):
        step = src.shape[0] // pieces
        for i in range(pieces):
            at = pl.ds(i * step, step)
            stores.append(pltpu.make_async_copy(src.at[at], dst.at[at], sems.at[len(stores)]))
    for c in stores:
        c.start()
    for c in stores:
        c.wait()


def place(*arrays):
    pieces = 4
    return pl.pallas_call(
        functools.partial(place_kernel, pieces),
        out_shape=tuple(jax.ShapeDtypeStruct(a.shape, a.dtype) for a in arrays),
        in_specs=[pl.BlockSpec(memory_space=pltpu.VMEM)] * len(arrays),
        out_specs=(pl.BlockSpec(memory_space=pl.ANY),) * len(arrays),
        scratch_shapes=[pltpu.SemaphoreType.DMA((pieces * len(arrays),))],
        compiler_params=pltpu.CompilerParams(vmem_limit_bytes=4 * 1024 * 1024),
        name="place",
    )(*arrays)


def body(n_dp, n_exp, saved_inputs, saved_grads, row_counts, row_seq, proj_in, proj_out):
    cap, width = saved_inputs.shape[2:]
    ff = saved_grads.shape[3]
    rank = proj_in.shape[1]
    square = rank * rank
    lanes = 128
    lo = 2 if n_dp % 2 == 0 else 1
    hi = n_dp // lo
    share = SEQ_DEV // n_exp
    rows = cap // CHUNKS
    msgs = CHUNKS + 1
    vmem = pl.BlockSpec(memory_space=pltpu.VMEM)
    hbm = pl.BlockSpec(memory_space=pl.ANY)
    logged, fisher = pl.pallas_call(
        functools.partial(kernel, n_dp, n_exp, lo),
        out_shape=(
            pltpu.VMEM((n_exp, share, square), jnp.bfloat16),
            pltpu.VMEM((square // n_dp * square // lanes, lanes), jnp.float32),
        ),
        in_specs=[pl.BlockSpec(memory_space=pltpu.SMEM), vmem, hbm, hbm, hbm, hbm],
        out_specs=(hbm, vmem),
        scratch_shapes=[
            pltpu.VMEM((cap, width), jnp.bfloat16),
            pltpu.VMEM((cap, ff), jnp.bfloat16),
            pltpu.VMEM((rank, width), jnp.bfloat16),
            pltpu.VMEM((rank, ff), jnp.bfloat16),
            pltpu.VMEM((width, lanes), jnp.bfloat16),
            pltpu.VMEM((ff, lanes), jnp.bfloat16),
            pltpu.VMEM((hi * CHUNKS, 2 * rank, rows), jnp.bfloat16),
            pltpu.VMEM((hi, cap // lanes, lanes), jnp.int32),
            pltpu.VMEM((square, cap), jnp.bfloat16),
            pltpu.VMEM((SEQ_DEV, cap), jnp.bfloat16),
            pltpu.VMEM((square, SEQ_DEV), jnp.bfloat16),
            pltpu.VMEM((SEQ_DEV, square), jnp.bfloat16),
            pltpu.VMEM((square // hi, square), jnp.float32),
            pltpu.VMEM((lo, square // n_dp, square), jnp.bfloat16),
            pltpu.VMEM((lo, square // n_dp, square), jnp.bfloat16),
            pltpu.VMEM((lo, cap // lanes, lanes), jnp.float32),
            pltpu.SemaphoreType.DMA((2 * CHUNKS,)),
            pltpu.SemaphoreType.DMA((2,)),
            pltpu.SemaphoreType.DMA(((hi - 1) * msgs,)),
            pltpu.SemaphoreType.DMA((hi * msgs,)),
            pltpu.SemaphoreType.DMA((n_exp - 1,)),
            pltpu.SemaphoreType.DMA((n_exp - 1,)),
            pltpu.SemaphoreType.DMA((max(lo - 1, 1) * (PIECES + 1),)),
            pltpu.SemaphoreType.DMA((max(lo - 1, 1) * (PIECES + 1),)),
            pltpu.SemaphoreType.DMA,
        ],
        compiler_params=pltpu.CompilerParams(
            collective_id=0, has_side_effects=True, vmem_limit_bytes=56 * 1024 * 1024
        ),
    )(
        row_counts,
        row_seq.reshape(cap // lanes, lanes),
        saved_inputs.reshape(cap, width),
        saved_grads.reshape(cap, ff),
        proj_in.T,
        proj_out.T,
    )
    logged, fisher = place(logged, fisher)
    return logged, fisher.reshape(square // n_dp, 1, square)


def solution(mesh):
    in_specs = (
        P("dp", "expert", None, None),
        P("dp", "expert", None, None),
        P("dp", "expert"),
        P("dp", "expert", None),
        P(),
        P(),
    )
    out_specs = (P(None, ("dp", "expert"), None), P("dp", "expert", None))
    return jax.shard_map(
        functools.partial(body, mesh.shape["dp"], mesh.shape["expert"]),
        mesh=mesh,
        in_specs=in_specs,
        out_specs=out_specs,
        check_vma=False,
    )
```

```python
import functools

import jax
import jax.numpy as jnp
from jax import lax
from jax.experimental import pallas as pl
from jax.experimental.pallas import tpu as pltpu
from jax.sharding import PartitionSpec as P

SEQ_DEV = 256
CHUNKS = 4
AHEAD = 2
PIECES = 2
MESH = pl.DeviceIdType.MESH
NT = (((1,), (1,)), ((), ()))


def kernel(
    n_dp,
    n_exp,
    lo,
    count_ref,
    seq_ref,
    x_hbm,
    g_hbm,
    pin_hbm,
    pout_hbm,
    logged_ref,
    fisher_ref,
    xb,
    gb,
    pin,
    pout,
    wide_in,
    wide_out,
    fac,
    seqs,
    outer,
    onehot,
    gt,
    lg,
    acc,
    give,
    got,
    lives,
    in_sem,
    p_sem,
    send_sem,
    recv_sem,
    lsend_sem,
    lrecv_sem,
    xsend_sem,
    xrecv_sem,
    local_sem,
):
    hi = n_dp // lo
    msgs = CHUNKS + 1
    rank = pin_hbm.shape[0]
    cap = x_hbm.shape[0]
    rows = cap // CHUNKS
    lanes = seq_ref.shape[1]
    share = SEQ_DEV // n_exp
    fb = acc.shape[0] // lo

    dp = lax.axis_index("dp")
    ex = lax.axis_index("expert")
    z = dp // lo
    x = dp % lo

    p_copies = [
        pltpu.make_async_copy(pin_hbm, pin, p_sem.at[0]),
        pltpu.make_async_copy(pout_hbm, pout, p_sem.at[1]),
    ]
    for c in p_copies:
        c.start()

    def load(ch):
        at = pl.ds(pl.multiple_of(ch * rows, rows), rows) if not isinstance(ch, int) else pl.ds(ch * rows, rows)
        return (
            pltpu.make_async_copy(x_hbm.at[at], xb.at[at], in_sem.at[2 * ch]),
            pltpu.make_async_copy(g_hbm.at[at], gb.at[at], in_sem.at[2 * ch + 1]),
        )

    for ch in range(AHEAD):
        for c in load(ch):
            c.start()

    barrier = pltpu.get_barrier_semaphore()

    def greet(device):
        pl.semaphore_signal(barrier, inc=1, device_id=device, device_id_type=MESH)

    for s in range(1, lo):
        greet((z * lo + lax.rem(x + s, lo), ex))
    for s in range(1, n_exp):
        greet((dp, lax.rem(ex + s, n_exp)))

    for s in range(1, hi):
        greet((lax.rem(z + s, hi) * lo + x, ex))

    def copy_of(src, m, s):
        ref = seqs.at[src] if isinstance(m, int) and m == 0 else fac.at[src * CHUNKS + (m - 1)]
        return pltpu.make_async_remote_copy(
            src_ref=ref,
            dst_ref=ref,
            send_sem=send_sem.at[(s - 1) * msgs + m],
            recv_sem=recv_sem.at[src * msgs + m],
            device_id=(lax.rem(z + s, hi) * lo + x, ex),
            device_id_type=MESH,
        )

    def send(m):
        for s in range(1, hi):
            copy_of(z, m, s).start()

    slot = (
        lax.broadcasted_iota(jnp.int32, seq_ref.shape, 0) * lanes
        + lax.broadcasted_iota(jnp.int32, seq_ref.shape, 1)
    )
    seqs[z] = jnp.where(slot < count_ref[0, 0], seq_ref[...], -1)

    for c in p_copies:
        c.wait()
    for src, dst in ((pin, wide_in), (pout, wide_out)):
        depth = dst.shape[0]
        groups = src.shape[1] // depth
        tall = [src[:, i * depth : (i + 1) * depth].astype(jnp.float32) for i in range(groups)]
        if groups * rank < lanes:
            tall.append(jnp.zeros((lanes - groups * rank, depth), jnp.float32))
        dst[...] = jnp.concatenate(tall, axis=0).T.astype(jnp.bfloat16)

    pl.semaphore_wait(barrier, (lo - 1) + (n_exp - 1) + (hi - 1))
    send(0)
    group = lax.broadcasted_iota(jnp.int32, (rows, lanes), 1) // rank

    def project(buf, wide, at):
        depth = wide.shape[0]
        groups = buf.shape[1] // depth
        total = jnp.zeros((rows, lanes), jnp.float32)
        for i in range(groups):
            part = jnp.dot(
                buf[at, i * depth : (i + 1) * depth], wide[...], preferred_element_type=jnp.float32
            )
            total = jnp.where(group == i, part, total)
        turned = total.T
        out = turned[:rank]
        for i in range(1, groups):
            out += turned[i * rank : (i + 1) * rank]
        return out.astype(jnp.bfloat16)

    def chunk(ch, carry):
        for c in load(ch):
            c.wait()

        @pl.when(ch + AHEAD < CHUNKS)
        def _():
            for c in load(ch + AHEAD):
                c.start()

        at = pl.ds(pl.multiple_of(ch * rows, rows), rows)
        mine = z * CHUNKS + ch
        fac[mine, :rank] = project(xb, wide_in, at)
        fac[mine, rank:] = project(gb, wide_out, at)
        send(ch + 1)
        return carry

    lax.fori_loop(0, CHUNKS, chunk, 0)

    def build(blk):
        for ch in range(CHUNKS):
            at = pl.ds(ch * rows, rows)
            f = fac[blk * CHUNKS + ch]
            wide = f[rank:].astype(jnp.float32)
            for k in range(rank):
                row = jnp.broadcast_to(wide[k : k + 1], (16, rows)).astype(jnp.bfloat16)
                for h in range(0, rank, 16):
                    outer[k * rank + h : k * rank + h + 16, at] = row * f[h : h + 16]
        ids = seqs[blk]
        want = lax.broadcasted_iota(jnp.int32, (SEQ_DEV, lanes), 0)
        for c in range(cap // lanes):
            onehot[:, c * lanes : (c + 1) * lanes] = jnp.where(
                want == ids[c : c + 1], 1.0, 0.0
            ).astype(jnp.bfloat16)

    def gram():
        gt[...] = lax.dot_general(
            outer[...], onehot[...], NT, preferred_element_type=jnp.float32
        ).astype(jnp.bfloat16)
        mine = gt[pl.ds(pl.multiple_of(z * lo * fb, lo * fb), lo * fb), :]
        return lax.dot_general(mine, gt[...], NT, preferred_element_type=jnp.float32)

    def rows_of(e):
        return lg.at[pl.ds(pl.multiple_of(e * share, share), share)]

    def log_copy(s):
        to = lax.rem(ex + s, n_exp)
        return pltpu.make_async_remote_copy(
            src_ref=rows_of(to),
            dst_ref=logged_ref.at[ex],
            send_sem=lsend_sem.at[s - 1],
            recv_sem=lrecv_sem.at[s - 1],
            device_id=(dp, to),
            device_id_type=MESH,
        )

    keep = pltpu.make_async_copy(rows_of(ex), logged_ref.at[ex], local_sem)
    acc[...] = jnp.zeros_like(acc)

    def block(t, carry):
        d = (t + 1) // 2
        sz = z + d * (2 * lax.rem(t, 2) - 1)

        @pl.when((sz >= 0) & (sz < hi))
        def _():
            @pl.when(t > 0)
            def _():
                for m in range(msgs):
                    copy_of(sz, m, 1).wait_recv()

            build(sz)

            @pl.when(t == 0)
            def _():
                lg[...] = lax.dot_general(
                    onehot[...], outer[...], NT, preferred_element_type=jnp.float32
                ).astype(jnp.bfloat16)
                for s in range(1, n_exp):
                    log_copy(s).start()
                keep.start()

            acc[...] += gram()

        return carry

    lax.fori_loop(0, 2 * hi - 1, block, 0)

    live = jnp.zeros(seq_ref.shape, jnp.float32)
    for p in range(hi):
        live += jnp.where(seqs[p] >= 0, 1.0, 0.0)
    lives[0] = live

    piece = fb // PIECES

    def rows_at(q):
        return pl.ds(q * piece, piece)

    def across(s, q):
        to = z * lo + lax.rem(x + s, lo)
        k = (s - 1) * (PIECES + 1) + q + 1
        src, dst = (lives.at[0], lives.at[s]) if q < 0 else (
            give.at[s, rows_at(q)],
            got.at[s, rows_at(q)],
        )
        return pltpu.make_async_remote_copy(
            src_ref=src,
            dst_ref=dst,
            send_sem=xsend_sem.at[k],
            recv_sem=xrecv_sem.at[k],
            device_id=(to, ex),
            device_id_type=MESH,
        )

    for s in range(1, lo):
        across(s, -1).start()
        theirs = lax.rem(x + s, lo) * fb
        for q in range(PIECES):
            at = pl.ds(pl.multiple_of(theirs + q * piece, piece), piece)
            give[s, rows_at(q)] = acc[at].astype(jnp.bfloat16)
            across(s, q).start()
    for s in range(1, lo):
        across(s, -1).wait_recv()
        live += lives[s]
    scale = 1.0 / jnp.sum(live)
    tiles = acc.shape[1] // lanes
    for q in range(PIECES):
        at = pl.ds(pl.multiple_of(x * fb + q * piece, piece), piece)
        total = acc[at]
        for s in range(1, lo):
            across(s, q).wait_recv()
            total += got[s, rows_at(q)].astype(jnp.float32)
        total *= scale
        for c in range(tiles):
            fisher_ref[pl.ds(q * piece * tiles + c, piece, stride=tiles), :] = total[
                :, c * lanes : (c + 1) * lanes
            ]

    for s in range(1, hi):
        for m in range(msgs):
            copy_of(z, m, s).wait_send()
    for s in range(1, lo):
        for q in range(-1, PIECES):
            across(s, q).wait_send()
    keep.wait()
    for s in range(1, n_exp):
        log_copy(s).wait()


def groups_of(depth, rank):
    for groups in (4, 3, 2):
        if groups * rank <= 128 and depth % (groups * 256) == 0:
            return groups
    return 1


def place_kernel(pieces, *refs):
    sems = refs[-1]
    n = len(refs) // 2
    stores = []
    for src, dst in zip(refs[:n], refs[n:-1]):
        step = src.shape[0] // pieces
        for i in range(pieces):
            at = pl.ds(i * step, step)
            stores.append(pltpu.make_async_copy(src.at[at], dst.at[at], sems.at[len(stores)]))
    for c in stores:
        c.start()
    for c in stores:
        c.wait()


def place(*arrays):
    pieces = 4
    return pl.pallas_call(
        functools.partial(place_kernel, pieces),
        out_shape=tuple(jax.ShapeDtypeStruct(a.shape, a.dtype) for a in arrays),
        in_specs=[pl.BlockSpec(memory_space=pltpu.VMEM)] * len(arrays),
        out_specs=(pl.BlockSpec(memory_space=pl.ANY),) * len(arrays),
        scratch_shapes=[pltpu.SemaphoreType.DMA((pieces * len(arrays),))],
        compiler_params=pltpu.CompilerParams(vmem_limit_bytes=4 * 1024 * 1024),
        name="place",
    )(*arrays)


def body(n_dp, n_exp, saved_inputs, saved_grads, row_counts, row_seq, proj_in, proj_out):
    cap, width = saved_inputs.shape[2:]
    ff = saved_grads.shape[3]
    rank = proj_in.shape[1]
    square = rank * rank
    lanes = 128
    lo = 2 if n_dp % 2 == 0 else 1
    hi = n_dp // lo
    share = SEQ_DEV // n_exp
    rows = cap // CHUNKS
    msgs = CHUNKS + 1
    vmem = pl.BlockSpec(memory_space=pltpu.VMEM)
    hbm = pl.BlockSpec(memory_space=pl.ANY)
    logged, fisher = pl.pallas_call(
        functools.partial(kernel, n_dp, n_exp, lo),
        out_shape=(
            pltpu.VMEM((n_exp, share, square), jnp.bfloat16),
            pltpu.VMEM((square // n_dp * square // lanes, lanes), jnp.float32),
        ),
        in_specs=[pl.BlockSpec(memory_space=pltpu.SMEM), vmem, hbm, hbm, hbm, hbm],
        out_specs=(hbm, vmem),
        scratch_shapes=[
            pltpu.VMEM((cap, width), jnp.bfloat16),
            pltpu.VMEM((cap, ff), jnp.bfloat16),
            pltpu.VMEM((rank, width), jnp.bfloat16),
            pltpu.VMEM((rank, ff), jnp.bfloat16),
            pltpu.VMEM((width // groups_of(width, rank), lanes), jnp.bfloat16),
            pltpu.VMEM((ff // groups_of(ff, rank), lanes), jnp.bfloat16),
            pltpu.VMEM((hi * CHUNKS, 2 * rank, rows), jnp.bfloat16),
            pltpu.VMEM((hi, cap // lanes, lanes), jnp.int32),
            pltpu.VMEM((square, cap), jnp.bfloat16),
            pltpu.VMEM((SEQ_DEV, cap), jnp.bfloat16),
            pltpu.VMEM((square, SEQ_DEV), jnp.bfloat16),
            pltpu.VMEM((SEQ_DEV, square), jnp.bfloat16),
            pltpu.VMEM((square // hi, square), jnp.float32),
            pltpu.VMEM((lo, square // n_dp, square), jnp.bfloat16),
            pltpu.VMEM((lo, square // n_dp, square), jnp.bfloat16),
            pltpu.VMEM((lo, cap // lanes, lanes), jnp.float32),
            pltpu.SemaphoreType.DMA((2 * CHUNKS,)),
            pltpu.SemaphoreType.DMA((2,)),
            pltpu.SemaphoreType.DMA(((hi - 1) * msgs,)),
            pltpu.SemaphoreType.DMA((hi * msgs,)),
            pltpu.SemaphoreType.DMA((n_exp - 1,)),
            pltpu.SemaphoreType.DMA((n_exp - 1,)),
            pltpu.SemaphoreType.DMA((max(lo - 1, 1) * (PIECES + 1),)),
            pltpu.SemaphoreType.DMA((max(lo - 1, 1) * (PIECES + 1),)),
            pltpu.SemaphoreType.DMA,
        ],
        compiler_params=pltpu.CompilerParams(
            collective_id=0, has_side_effects=True, vmem_limit_bytes=56 * 1024 * 1024
        ),
    )(
        row_counts,
        row_seq.reshape(cap // lanes, lanes),
        saved_inputs.reshape(cap, width),
        saved_grads.reshape(cap, ff),
        proj_in.T,
        proj_out.T,
    )
    logged, fisher = place(logged, fisher)
    return logged, fisher.reshape(square // n_dp, 1, square)


def solution(mesh):
    in_specs = (
        P("dp", "expert", None, None),
        P("dp", "expert", None, None),
        P("dp", "expert"),
        P("dp", "expert", None),
        P(),
        P(),
    )
    out_specs = (P(None, ("dp", "expert"), None), P("dp", "expert", None))
    return jax.shard_map(
        functools.partial(body, mesh.shape["dp"], mesh.shape["expert"]),
        mesh=mesh,
        in_specs=in_specs,
        out_specs=out_specs,
        check_vma=False,
    )
```

```python
import functools

import jax
import jax.numpy as jnp
from jax import lax
from jax.experimental import pallas as pl
from jax.experimental.pallas import tpu as pltpu
from jax.sharding import PartitionSpec as P

SEQ_DEV = 256
CHUNKS = 4
AHEAD = 2
PIECES = 2
MESH = pl.DeviceIdType.MESH
NT = (((1,), (1,)), ((), ()))


def kernel(
    n_dp,
    n_exp,
    lo,
    count_ref,
    seq_ref,
    x_hbm,
    g_hbm,
    pin_hbm,
    pout_hbm,
    logged_ref,
    fisher_ref,
    xb,
    gb,
    pin,
    pout,
    wide_in,
    wide_out,
    fac,
    seqs,
    outer,
    onehot,
    gt,
    lg,
    acc,
    give,
    got,
    lives,
    in_sem,
    p_sem,
    send_sem,
    recv_sem,
    lsend_sem,
    lrecv_sem,
    xsend_sem,
    xrecv_sem,
    fsend_sem,
    frecv_sem,
    local_sem,
):
    hi = n_dp // lo
    msgs = CHUNKS + 1
    rank = pin_hbm.shape[0]
    cap = x_hbm.shape[0]
    rows = cap // CHUNKS
    lanes = seq_ref.shape[1]
    share = SEQ_DEV // n_exp
    fb = acc.shape[0] // lo

    dp = lax.axis_index("dp")
    ex = lax.axis_index("expert")
    z = dp // lo
    x = dp % lo

    p_copies = [
        pltpu.make_async_copy(pin_hbm, pin, p_sem.at[0]),
        pltpu.make_async_copy(pout_hbm, pout, p_sem.at[1]),
    ]
    for c in p_copies:
        c.start()

    def load(ch):
        at = pl.ds(pl.multiple_of(ch * rows, rows), rows) if not isinstance(ch, int) else pl.ds(ch * rows, rows)
        return (
            pltpu.make_async_copy(x_hbm.at[at], xb.at[at], in_sem.at[2 * ch]),
            pltpu.make_async_copy(g_hbm.at[at], gb.at[at], in_sem.at[2 * ch + 1]),
        )

    for ch in range(AHEAD):
        for c in load(ch):
            c.start()

    barrier = pltpu.get_barrier_semaphore()

    def greet(device):
        pl.semaphore_signal(barrier, inc=1, device_id=device, device_id_type=MESH)

    for s in range(1, lo):
        greet((z * lo + lax.rem(x + s, lo), ex))
    for s in range(1, n_exp):
        greet((dp, lax.rem(ex + s, n_exp)))

    for s in range(1, hi):
        greet((lax.rem(z + s, hi) * lo + x, ex))

    def copy_of(src, m, s):
        ref = seqs.at[src] if isinstance(m, int) and m == 0 else fac.at[src * CHUNKS + (m - 1)]
        return pltpu.make_async_remote_copy(
            src_ref=ref,
            dst_ref=ref,
            send_sem=send_sem.at[(s - 1) * msgs + m],
            recv_sem=recv_sem.at[src * msgs + m],
            device_id=(lax.rem(z + s, hi) * lo + x, ex),
            device_id_type=MESH,
        )

    def send(m):
        for s in range(1, hi):
            copy_of(z, m, s).start()

    slot = (
        lax.broadcasted_iota(jnp.int32, seq_ref.shape, 0) * lanes
        + lax.broadcasted_iota(jnp.int32, seq_ref.shape, 1)
    )
    seqs[z] = jnp.where(slot < count_ref[0, 0], seq_ref[...], -1)

    for c in p_copies:
        c.wait()
    for src, dst in ((pin, wide_in), (pout, wide_out)):
        depth = dst.shape[0]
        groups = src.shape[1] // depth
        tall = [src[:, i * depth : (i + 1) * depth].astype(jnp.float32) for i in range(groups)]
        if groups * rank < lanes:
            tall.append(jnp.zeros((lanes - groups * rank, depth), jnp.float32))
        dst[...] = jnp.concatenate(tall, axis=0).T.astype(jnp.bfloat16)

    pl.semaphore_wait(barrier, (lo - 1) + (n_exp - 1) + (hi - 1))
    send(0)
    group = lax.broadcasted_iota(jnp.int32, (rows, lanes), 1) // rank

    def project(buf, wide, at):
        depth = wide.shape[0]
        groups = buf.shape[1] // depth
        total = jnp.zeros((rows, lanes), jnp.float32)
        for i in range(groups):
            part = jnp.dot(
                buf[at, i * depth : (i + 1) * depth], wide[...], preferred_element_type=jnp.float32
            )
            total = jnp.where(group == i, part, total)
        turned = total.T
        out = turned[:rank]
        for i in range(1, groups):
            out += turned[i * rank : (i + 1) * rank]
        return out.astype(jnp.bfloat16)

    def chunk(ch, carry):
        for c in load(ch):
            c.wait()

        @pl.when(ch + AHEAD < CHUNKS)
        def _():
            for c in load(ch + AHEAD):
                c.start()

        at = pl.ds(pl.multiple_of(ch * rows, rows), rows)
        mine = z * CHUNKS + ch
        fac[mine, :rank] = project(xb, wide_in, at)
        fac[mine, rank:] = project(gb, wide_out, at)
        send(ch + 1)
        return carry

    lax.fori_loop(0, CHUNKS, chunk, 0)

    def build(blk):
        for ch in range(CHUNKS):
            at = pl.ds(ch * rows, rows)
            f = fac[blk * CHUNKS + ch]
            wide = f[rank:].astype(jnp.float32)
            for k in range(rank):
                row = jnp.broadcast_to(wide[k : k + 1], (16, rows)).astype(jnp.bfloat16)
                for h in range(0, rank, 16):
                    outer[k * rank + h : k * rank + h + 16, at] = row * f[h : h + 16]
        ids = seqs[blk]
        want = lax.broadcasted_iota(jnp.int32, (SEQ_DEV, lanes), 0)
        for c in range(cap // lanes):
            onehot[:, c * lanes : (c + 1) * lanes] = jnp.where(
                want == ids[c : c + 1], 1.0, 0.0
            ).astype(jnp.bfloat16)

    def gram():
        gt[...] = lax.dot_general(
            outer[...], onehot[...], NT, preferred_element_type=jnp.float32
        ).astype(jnp.bfloat16)
        mine = gt[pl.ds(pl.multiple_of(z * lo * fb, lo * fb), lo * fb), :]
        return lax.dot_general(mine, gt[...], NT, preferred_element_type=jnp.float32)

    def rows_of(e):
        return lg.at[pl.ds(pl.multiple_of(e * share, share), share)]

    def log_copy(s):
        to = lax.rem(ex + s, n_exp)
        return pltpu.make_async_remote_copy(
            src_ref=rows_of(to),
            dst_ref=logged_ref.at[ex],
            send_sem=lsend_sem.at[s - 1],
            recv_sem=lrecv_sem.at[s - 1],
            device_id=(dp, to),
            device_id_type=MESH,
        )

    keep = pltpu.make_async_copy(rows_of(ex), logged_ref.at[ex], local_sem)
    acc[...] = jnp.zeros_like(acc)
    lives[0] = jnp.zeros(seq_ref.shape, jnp.float32)

    far = jnp.where(2 * z < hi, hi - 1, 0)

    def block(t, carry):
        d = (t + 1) // 2
        sz = z + d * (2 * lax.rem(t, 2) - 1)

        @pl.when((sz >= 0) & (sz < hi) & (sz != far))
        def _():
            @pl.when(t > 0)
            def _():
                for m in range(msgs):
                    copy_of(sz, m, 1).wait_recv()

            build(sz)
            lives[0] += jnp.where(seqs[sz] >= 0, 1.0, 0.0)

            @pl.when(t == 0)
            def _():
                lg[...] = lax.dot_general(
                    onehot[...], outer[...], NT, preferred_element_type=jnp.float32
                ).astype(jnp.bfloat16)
                for s in range(1, n_exp):
                    log_copy(s).start()
                keep.start()

            acc[...] += gram()

        return carry

    lax.fori_loop(0, 2 * hi - 1, block, 0)

    live = lives[0]

    piece = fb // PIECES

    def rows_at(q):
        return pl.ds(q * piece, piece)

    def across(s, q):
        to = z * lo + lax.rem(x + s, lo)
        k = (s - 1) * (PIECES + 1) + q + 1
        src, dst = (lives.at[0], lives.at[s]) if q < 0 else (
            give.at[s, rows_at(q)],
            got.at[s, rows_at(q)],
        )
        return pltpu.make_async_remote_copy(
            src_ref=src,
            dst_ref=dst,
            send_sem=xsend_sem.at[k],
            recv_sem=xrecv_sem.at[k],
            device_id=(to, ex),
            device_id_type=MESH,
        )

    for s in range(1, lo):
        across(s, -1).start()
        theirs = lax.rem(x + s, lo) * fb
        for q in range(PIECES):
            at = pl.ds(pl.multiple_of(theirs + q * piece, piece), piece)
            give[s, rows_at(q)] = acc[at].astype(jnp.bfloat16)
            across(s, q).start()
    def pass_on(s, m):
        to = z * lo + lax.rem(x + s, lo)
        spare = hi + s - 1
        if m == 0:
            src, dst = seqs.at[far], seqs.at[spare]
        else:
            src, dst = fac.at[far * CHUNKS + m - 1], fac.at[spare * CHUNKS + m - 1]
        return pltpu.make_async_remote_copy(
            src_ref=src,
            dst_ref=dst,
            send_sem=fsend_sem.at[(s - 1) * msgs + m],
            recv_sem=frecv_sem.at[(s - 1) * msgs + m],
            device_id=(to, ex),
            device_id_type=MESH,
        )

    for m in range(msgs):
        copy_of(far, m, 1).wait_recv()
        for s in range(1, lo):
            pass_on(s, m).start()

    build(far)
    acc[...] += gram()
    live += jnp.where(seqs[far] >= 0, 1.0, 0.0)
    for s in range(1, lo):
        for m in range(msgs):
            pass_on(s, m).wait_recv()
        build(hi + s - 1)
        acc[...] += gram()
        across(s, -1).wait_recv()
        live += lives[s] + jnp.where(seqs[hi + s - 1] >= 0, 1.0, 0.0)
    scale = 1.0 / jnp.sum(live)
    tiles = acc.shape[1] // lanes
    for q in range(PIECES):
        at = pl.ds(pl.multiple_of(x * fb + q * piece, piece), piece)
        total = acc[at]
        for s in range(1, lo):
            across(s, q).wait_recv()
            total += got[s, rows_at(q)].astype(jnp.float32)
        total *= scale
        for c in range(tiles):
            fisher_ref[pl.ds(q * piece * tiles + c, piece, stride=tiles), :] = total[
                :, c * lanes : (c + 1) * lanes
            ]

    for s in range(1, hi):
        for m in range(msgs):
            copy_of(z, m, s).wait_send()
    for s in range(1, lo):
        for q in range(-1, PIECES):
            across(s, q).wait_send()
        for m in range(msgs):
            pass_on(s, m).wait_send()
    keep.wait()
    for s in range(1, n_exp):
        log_copy(s).wait()


def groups_of(depth, rank):
    for groups in (4, 3, 2):
        if groups * rank <= 128 and depth % (groups * 256) == 0:
            return groups
    return 1


def place_kernel(pieces, *refs):
    sems = refs[-1]
    n = len(refs) // 2
    stores = []
    for src, dst in zip(refs[:n], refs[n:-1]):
        step = src.shape[0] // pieces
        for i in range(pieces):
            at = pl.ds(i * step, step)
            stores.append(pltpu.make_async_copy(src.at[at], dst.at[at], sems.at[len(stores)]))
    for c in stores:
        c.start()
    for c in stores:
        c.wait()


def place(*arrays):
    pieces = 4
    return pl.pallas_call(
        functools.partial(place_kernel, pieces),
        out_shape=tuple(jax.ShapeDtypeStruct(a.shape, a.dtype) for a in arrays),
        in_specs=[pl.BlockSpec(memory_space=pltpu.VMEM)] * len(arrays),
        out_specs=(pl.BlockSpec(memory_space=pl.ANY),) * len(arrays),
        scratch_shapes=[pltpu.SemaphoreType.DMA((pieces * len(arrays),))],
        compiler_params=pltpu.CompilerParams(vmem_limit_bytes=4 * 1024 * 1024),
        name="place",
    )(*arrays)


def body(n_dp, n_exp, saved_inputs, saved_grads, row_counts, row_seq, proj_in, proj_out):
    cap, width = saved_inputs.shape[2:]
    ff = saved_grads.shape[3]
    rank = proj_in.shape[1]
    square = rank * rank
    lanes = 128
    lo = 2 if n_dp % 2 == 0 else 1
    hi = n_dp // lo
    share = SEQ_DEV // n_exp
    rows = cap // CHUNKS
    msgs = CHUNKS + 1
    vmem = pl.BlockSpec(memory_space=pltpu.VMEM)
    hbm = pl.BlockSpec(memory_space=pl.ANY)
    logged, fisher = pl.pallas_call(
        functools.partial(kernel, n_dp, n_exp, lo),
        out_shape=(
            pltpu.VMEM((n_exp, share, square), jnp.bfloat16),
            pltpu.VMEM((square // n_dp * square // lanes, lanes), jnp.float32),
        ),
        in_specs=[pl.BlockSpec(memory_space=pltpu.SMEM), vmem, hbm, hbm, hbm, hbm],
        out_specs=(hbm, vmem),
        scratch_shapes=[
            pltpu.VMEM((cap, width), jnp.bfloat16),
            pltpu.VMEM((cap, ff), jnp.bfloat16),
            pltpu.VMEM((rank, width), jnp.bfloat16),
            pltpu.VMEM((rank, ff), jnp.bfloat16),
            pltpu.VMEM((width // groups_of(width, rank), lanes), jnp.bfloat16),
            pltpu.VMEM((ff // groups_of(ff, rank), lanes), jnp.bfloat16),
            pltpu.VMEM(((hi + lo - 1) * CHUNKS, 2 * rank, rows), jnp.bfloat16),
            pltpu.VMEM((hi + lo - 1, cap // lanes, lanes), jnp.int32),
            pltpu.VMEM((square, cap), jnp.bfloat16),
            pltpu.VMEM((SEQ_DEV, cap), jnp.bfloat16),
            pltpu.VMEM((square, SEQ_DEV), jnp.bfloat16),
            pltpu.VMEM((SEQ_DEV, square), jnp.bfloat16),
            pltpu.VMEM((square // hi, square), jnp.float32),
            pltpu.VMEM((lo, square // n_dp, square), jnp.bfloat16),
            pltpu.VMEM((lo, square // n_dp, square), jnp.bfloat16),
            pltpu.VMEM((lo, cap // lanes, lanes), jnp.float32),
            pltpu.SemaphoreType.DMA((2 * CHUNKS,)),
            pltpu.SemaphoreType.DMA((2,)),
            pltpu.SemaphoreType.DMA(((hi - 1) * msgs,)),
            pltpu.SemaphoreType.DMA((hi * msgs,)),
            pltpu.SemaphoreType.DMA((n_exp - 1,)),
            pltpu.SemaphoreType.DMA((n_exp - 1,)),
            pltpu.SemaphoreType.DMA((max(lo - 1, 1) * (PIECES + 1),)),
            pltpu.SemaphoreType.DMA((max(lo - 1, 1) * (PIECES + 1),)),
            pltpu.SemaphoreType.DMA((max(lo - 1, 1) * msgs,)),
            pltpu.SemaphoreType.DMA((max(lo - 1, 1) * msgs,)),
            pltpu.SemaphoreType.DMA,
        ],
        compiler_params=pltpu.CompilerParams(
            collective_id=0, has_side_effects=True, vmem_limit_bytes=56 * 1024 * 1024
        ),
    )(
        row_counts,
        row_seq.reshape(cap // lanes, lanes),
        saved_inputs.reshape(cap, width),
        saved_grads.reshape(cap, ff),
        proj_in.T,
        proj_out.T,
    )
    logged, fisher = place(logged, fisher)
    return logged, fisher.reshape(square // n_dp, 1, square)


def solution(mesh):
    in_specs = (
        P("dp", "expert", None, None),
        P("dp", "expert", None, None),
        P("dp", "expert"),
        P("dp", "expert", None),
        P(),
        P(),
    )
    out_specs = (P(None, ("dp", "expert"), None), P("dp", "expert", None))
    return jax.shard_map(
        functools.partial(body, mesh.shape["dp"], mesh.shape["expert"]),
        mesh=mesh,
        in_specs=in_specs,
        out_specs=out_specs,
        check_vma=False,
    )
```

```python
import functools

import jax
import jax.numpy as jnp
from jax import lax
from jax.experimental import pallas as pl
from jax.experimental.pallas import tpu as pltpu
from jax.sharding import PartitionSpec as P

SEQ_DEV = 256
CHUNKS = 4
AHEAD = 2
PIECES = 2
MESH = pl.DeviceIdType.MESH
NT = (((1,), (1,)), ((), ()))


def kernel(
    n_dp,
    n_exp,
    lo,
    count_ref,
    seq_ref,
    x_hbm,
    g_hbm,
    pin_hbm,
    pout_hbm,
    logged_ref,
    fisher_ref,
    xb,
    gb,
    pin,
    pout,
    wide_in,
    wide_out,
    fac,
    seqs,
    outer,
    onehot,
    gt,
    lg,
    acc,
    give,
    got,
    lives,
    in_sem,
    p_sem,
    send_sem,
    recv_sem,
    lsend_sem,
    lrecv_sem,
    xsend_sem,
    xrecv_sem,
    local_sem,
):
    hi = n_dp // lo
    msgs = CHUNKS + 1
    rank = pin_hbm.shape[0]
    cap = x_hbm.shape[0]
    rows = cap // CHUNKS
    lanes = seq_ref.shape[1]
    share = SEQ_DEV // n_exp
    fb = acc.shape[0] // lo

    dp = lax.axis_index("dp")
    ex = lax.axis_index("expert")
    z = dp // lo
    x = dp % lo

    p_copies = [
        pltpu.make_async_copy(pin_hbm, pin, p_sem.at[0]),
        pltpu.make_async_copy(pout_hbm, pout, p_sem.at[1]),
    ]
    for c in p_copies:
        c.start()

    def load(ch):
        at = pl.ds(ch * rows, rows)
        return (
            pltpu.make_async_copy(x_hbm.at[at], xb.at[at], in_sem.at[2 * ch]),
            pltpu.make_async_copy(g_hbm.at[at], gb.at[at], in_sem.at[2 * ch + 1]),
        )

    for ch in range(AHEAD):
        for c in load(ch):
            c.start()

    barrier = pltpu.get_barrier_semaphore()

    def greet(device):
        pl.semaphore_signal(barrier, inc=1, device_id=device, device_id_type=MESH)

    for s in range(1, lo):
        greet((z * lo + lax.rem(x + s, lo), ex))
    for s in range(1, n_exp):
        greet((dp, lax.rem(ex + s, n_exp)))

    for s in range(1, hi):
        greet((lax.rem(z + s, hi) * lo + x, ex))

    def copy_of(src, m, s):
        ref = seqs.at[src] if m == 0 else fac.at[src * CHUNKS + (m - 1)]
        return pltpu.make_async_remote_copy(
            src_ref=ref,
            dst_ref=ref,
            send_sem=send_sem.at[(s - 1) * msgs + m],
            recv_sem=recv_sem.at[src * msgs + m],
            device_id=(lax.rem(z + s, hi) * lo + x, ex),
            device_id_type=MESH,
        )

    def send(m):
        for s in range(1, hi):
            copy_of(z, m, s).start()

    slot = (
        lax.broadcasted_iota(jnp.int32, seq_ref.shape, 0) * lanes
        + lax.broadcasted_iota(jnp.int32, seq_ref.shape, 1)
    )
    seqs[z] = jnp.where(slot < count_ref[0, 0], seq_ref[...], -1)

    for c in p_copies:
        c.wait()
    for src, dst, before in ((pin, wide_in, 0), (pout, wide_out, rank)):
        blank = lambda r: [jnp.zeros((r, src.shape[1]), jnp.float32)] if r else []
        tall = blank(before) + [src[...].astype(jnp.float32)] + blank(lanes - rank - before)
        dst[...] = jnp.concatenate(tall, axis=0).T.astype(jnp.bfloat16)
    for ch in range(CHUNKS):
        for c in load(ch):
            c.wait()
        if ch + AHEAD < CHUNKS:
            for c in load(ch + AHEAD):
                c.start()
        at = pl.ds(ch * rows, rows)
        both = jnp.dot(xb[at], wide_in[...], preferred_element_type=jnp.float32)
        both += jnp.dot(gb[at], wide_out[...], preferred_element_type=jnp.float32)
        fac[z * CHUNKS + ch] = both.T[: 2 * rank].astype(jnp.bfloat16)
        if ch == 0:
            pl.semaphore_wait(barrier, (lo - 1) + (n_exp - 1) + (hi - 1))
            send(0)
        send(ch + 1)

    def build(blk):
        for ch in range(CHUNKS):
            at = pl.ds(ch * rows, rows)
            f = fac[blk * CHUNKS + ch]
            wide = f.astype(jnp.float32)
            low = wide[:rank]
            for k in range(rank):
                outer[k * rank : (k + 1) * rank, at] = (wide[rank + k : rank + k + 1] * low).astype(
                    jnp.bfloat16
                )
        ids = seqs[blk]
        want = lax.broadcasted_iota(jnp.int32, (SEQ_DEV, lanes), 0)
        for c in range(cap // lanes):
            onehot[:, c * lanes : (c + 1) * lanes] = jnp.where(
                want == ids[c : c + 1], 1.0, 0.0
            ).astype(jnp.bfloat16)

    def gram():
        gt[...] = lax.dot_general(
            outer[...], onehot[...], NT, preferred_element_type=jnp.float32
        ).astype(jnp.bfloat16)
        mine = gt[pl.ds(pl.multiple_of(z * lo * fb, lo * fb), lo * fb), :]
        return lax.dot_general(mine, gt[...], NT, preferred_element_type=jnp.float32)

    build(z)
    lg[...] = lax.dot_general(
        onehot[...], outer[...], NT, preferred_element_type=jnp.float32
    ).astype(jnp.bfloat16)

    def rows_of(e):
        return lg.at[pl.ds(pl.multiple_of(e * share, share), share)]

    def log_copy(s):
        to = lax.rem(ex + s, n_exp)
        return pltpu.make_async_remote_copy(
            src_ref=rows_of(to),
            dst_ref=logged_ref.at[ex],
            send_sem=lsend_sem.at[s - 1],
            recv_sem=lrecv_sem.at[s - 1],
            device_id=(dp, to),
            device_id_type=MESH,
        )

    for s in range(1, n_exp):
        log_copy(s).start()
    keep = pltpu.make_async_copy(rows_of(ex), logged_ref.at[ex], local_sem)
    keep.start()
    acc[...] = gram()

    def at_distance(d, carry):
        def one(side, carry):
            sz = z + d * (2 * side - 1)

            @pl.when((sz >= 0) & (sz < hi))
            def _():
                for m in range(msgs):
                    copy_of(sz, m, 1).wait_recv()
                build(sz)
                acc[...] += gram()

            return carry

        return lax.fori_loop(0, 2, one, carry)

    lax.fori_loop(1, hi, at_distance, 0)

    live = jnp.zeros(seq_ref.shape, jnp.float32)
    for p in range(hi):
        live += jnp.where(seqs[p] >= 0, 1.0, 0.0)
    lives[0] = live

    piece = fb // PIECES

    def rows_at(q):
        return pl.ds(q * piece, piece)

    def across(s, q):
        to = z * lo + lax.rem(x + s, lo)
        k = (s - 1) * (PIECES + 1) + q + 1
        src, dst = (lives.at[0], lives.at[s]) if q < 0 else (
            give.at[s, rows_at(q)],
            got.at[s, rows_at(q)],
        )
        return pltpu.make_async_remote_copy(
            src_ref=src,
            dst_ref=dst,
            send_sem=xsend_sem.at[k],
            recv_sem=xrecv_sem.at[k],
            device_id=(to, ex),
            device_id_type=MESH,
        )

    for s in range(1, lo):
        across(s, -1).start()
        theirs = lax.rem(x + s, lo) * fb
        for q in range(PIECES):
            at = pl.ds(pl.multiple_of(theirs + q * piece, piece), piece)
            give[s, rows_at(q)] = acc[at].astype(jnp.bfloat16)
            across(s, q).start()
    for s in range(1, lo):
        across(s, -1).wait_recv()
        live += lives[s]
    scale = 1.0 / jnp.sum(live)
    tiles = acc.shape[1] // lanes
    for q in range(PIECES):
        at = pl.ds(pl.multiple_of(x * fb + q * piece, piece), piece)
        total = acc[at]
        for s in range(1, lo):
            across(s, q).wait_recv()
            total += got[s, rows_at(q)].astype(jnp.float32)
        total *= scale
        for c in range(tiles):
            fisher_ref[pl.ds(q * piece * tiles + c, piece, stride=tiles), :] = total[
                :, c * lanes : (c + 1) * lanes
            ]

    for s in range(1, hi):
        for m in range(msgs):
            copy_of(z, m, s).wait_send()
    for s in range(1, lo):
        for q in range(-1, PIECES):
            across(s, q).wait_send()
    keep.wait()
    for s in range(1, n_exp):
        log_copy(s).wait()


def place_kernel(pieces, *refs):
    sems = refs[-1]
    n = len(refs) // 2
    stores = []
    for src, dst in zip(refs[:n], refs[n:-1]):
        step = src.shape[0] // pieces
        for i in range(pieces):
            at = pl.ds(i * step, step)
            stores.append(pltpu.make_async_copy(src.at[at], dst.at[at], sems.at[len(stores)]))
    for c in stores:
        c.start()
    for c in stores:
        c.wait()


def place(*arrays):
    pieces = 4
    return pl.pallas_call(
        functools.partial(place_kernel, pieces),
        out_shape=tuple(jax.ShapeDtypeStruct(a.shape, a.dtype) for a in arrays),
        in_specs=[pl.BlockSpec(memory_space=pltpu.VMEM)] * len(arrays),
        out_specs=(pl.BlockSpec(memory_space=pl.ANY),) * len(arrays),
        scratch_shapes=[pltpu.SemaphoreType.DMA((pieces * len(arrays),))],
        compiler_params=pltpu.CompilerParams(vmem_limit_bytes=4 * 1024 * 1024),
        name="place",
    )(*arrays)


def body(n_dp, n_exp, saved_inputs, saved_grads, row_counts, row_seq, proj_in, proj_out):
    cap, width = saved_inputs.shape[2:]
    ff = saved_grads.shape[3]
    rank = proj_in.shape[1]
    square = rank * rank
    lanes = 128
    lo = 2 if n_dp % 2 == 0 else 1
    hi = n_dp // lo
    share = SEQ_DEV // n_exp
    rows = cap // CHUNKS
    msgs = CHUNKS + 1
    vmem = pl.BlockSpec(memory_space=pltpu.VMEM)
    hbm = pl.BlockSpec(memory_space=pl.ANY)
    logged, fisher = pl.pallas_call(
        functools.partial(kernel, n_dp, n_exp, lo),
        out_shape=(
            pltpu.VMEM((n_exp, share, square), jnp.bfloat16),
            pltpu.VMEM((square // n_dp * square // lanes, lanes), jnp.float32),
        ),
        in_specs=[pl.BlockSpec(memory_space=pltpu.SMEM), vmem, hbm, hbm, hbm, hbm],
        out_specs=(hbm, vmem),
        scratch_shapes=[
            pltpu.VMEM((cap, width), jnp.bfloat16),
            pltpu.VMEM((cap, ff), jnp.bfloat16),
            pltpu.VMEM((rank, width), jnp.bfloat16),
            pltpu.VMEM((rank, ff), jnp.bfloat16),
            pltpu.VMEM((width, lanes), jnp.bfloat16),
            pltpu.VMEM((ff, lanes), jnp.bfloat16),
            pltpu.VMEM((hi * CHUNKS, 2 * rank, rows), jnp.bfloat16),
            pltpu.VMEM((hi, cap // lanes, lanes), jnp.int32),
            pltpu.VMEM((square, cap), jnp.bfloat16),
            pltpu.VMEM((SEQ_DEV, cap), jnp.bfloat16),
            pltpu.VMEM((square, SEQ_DEV), jnp.bfloat16),
            pltpu.VMEM((SEQ_DEV, square), jnp.bfloat16),
            pltpu.VMEM((square // hi, square), jnp.float32),
            pltpu.VMEM((lo, square // n_dp, square), jnp.bfloat16),
            pltpu.VMEM((lo, square // n_dp, square), jnp.bfloat16),
            pltpu.VMEM((lo, cap // lanes, lanes), jnp.float32),
            pltpu.SemaphoreType.DMA((2 * CHUNKS,)),
            pltpu.SemaphoreType.DMA((2,)),
            pltpu.SemaphoreType.DMA(((hi - 1) * msgs,)),
            pltpu.SemaphoreType.DMA((hi * msgs,)),
            pltpu.SemaphoreType.DMA((n_exp - 1,)),
            pltpu.SemaphoreType.DMA((n_exp - 1,)),
            pltpu.SemaphoreType.DMA((max(lo - 1, 1) * (PIECES + 1),)),
            pltpu.SemaphoreType.DMA((max(lo - 1, 1) * (PIECES + 1),)),
            pltpu.SemaphoreType.DMA,
        ],
        compiler_params=pltpu.CompilerParams(
            collective_id=0, has_side_effects=True, vmem_limit_bytes=56 * 1024 * 1024
        ),
    )(
        row_counts,
        row_seq.reshape(cap // lanes, lanes),
        saved_inputs.reshape(cap, width),
        saved_grads.reshape(cap, ff),
        proj_in.T,
        proj_out.T,
    )
    logged, fisher = place(logged, fisher)
    return logged, fisher.reshape(square // n_dp, 1, square)


def solution(mesh):
    in_specs = (
        P("dp", "expert", None, None),
        P("dp", "expert", None, None),
        P("dp", "expert"),
        P("dp", "expert", None),
        P(),
        P(),
    )
    out_specs = (P(None, ("dp", "expert"), None), P("dp", "expert", None))
    return jax.shard_map(
        functools.partial(body, mesh.shape["dp"], mesh.shape["expert"]),
        mesh=mesh,
        in_specs=in_specs,
        out_specs=out_specs,
        check_vma=False,
    )
```
